128 devices in a mesh: adapter: 8 (over x, core), row: 16 (over z, y).
Axes of the slice: x: 4, y: 4, z: 4, core: 2. Of those that a mesh axis runs over, the one named last changes fastest.
Arguments:
- up_factors_wide: bfloat16 [4096, 24576], P('row', 'adapter'), may hold values from -0.75 to 0.75
- transposed_down_factors: bfloat16 [4096, 24576], P('row', 'adapter'), may hold values from -0.75 to 0.75
- ranks: int32 [1536], P('adapter'), may hold values from 1 to 16
- initial_left_basis: float32 [4096, 256], P('row'), may hold values from -0.09375 to 0.09375
- initial_right_basis: float32 [4096, 256], P('row'), may hold values from -0.09375 to 0.09375
Outputs:
- fitted_u: float32 [4096, 256], P('row')
- fitted_v: float32 [4096, 256], P('row')
- cores: float32 [1536, 256, 256], P('adapter', 'row')
The draws below stay inside these ranges and needn't reach their ends.
All inputs are finite; a program needn't handle non-finite values.
Results may differ from the reference program's by a relative error of at most 0.012.
Values sent between devices are 32-bit elements; how exact they have to be, the bound alone decides.
No kernel may reach another device: no remote copies, remote signals or barrier semaphores. Data moves between devices by JAX's collectives and lax.ppermute only.
A program may use at most 128 MiB of HBM per device.

```python
import jax
import jax.numpy as jnp
from jax import lax

MODEL_WIDTH = 4096
K = 256
PADDED_RANK = 16
ITERS = 2
ADAPTER_TOTAL = 1536
N_ADAPTER = 8


def set_ends(array, stream_key, smallest, high):
    longest = array.shape.index(max(array.shape))
    spots = []
    for shift in (0, 1):
        where = [jax.random.randint(jax.random.fold_in(stream_key, axis), (), 0, length) for axis, length in enumerate(array.shape)]
        where[longest] = (where[longest] + shift) % array.shape[longest]
        spots.append(tuple(where))
    return array.at[spots[0]].set(smallest).at[spots[1]].set(high)


def level_of(stream_key, shape, cuts, smallest, high):
    loudness = 1.0
    for axis_at, parts in cuts:
        draws = jax.random.uniform(jax.random.fold_in(jax.random.fold_in(stream_key, 6), axis_at), (parts,), jnp.float32, smallest / len(cuts), high / len(cuts))
        loudness = loudness * jnp.repeat(jnp.exp(draws), shape[axis_at] // parts).reshape((-1,) + (1,) * (len(shape) - 1 - axis_at))
    return loudness


def centred(key, extent, scale, bound, cuts=(), kind=jnp.bfloat16):
    entries = jax.random.normal(key, extent, jnp.float32) * scale
    if len(cuts) > 0:
        entries = level_of(key, extent, cuts, -0.22, 0.18) * entries
    return jnp.clip(entries, min=-bound, max=bound).astype(kind)


def setup_inputs(seed: int = 0) -> dict:
    arg_keys = jax.random.split(jax.random.key(seed), 6)
    up_factors_wide = centred(arg_keys[0], (MODEL_WIDTH, ADAPTER_TOTAL * PADDED_RANK), 0.125, 0.75, ((0, 16), (1, 8)))
    transposed_down_factors = centred(arg_keys[1], (MODEL_WIDTH, ADAPTER_TOTAL * PADDED_RANK), 0.125, 0.75, ((0, 16), (1, 8)))
    ranks = set_ends(jax.random.randint(arg_keys[2], (ADAPTER_TOTAL,), 1, PADDED_RANK + 1), jax.random.fold_in(arg_keys[2], 1), 1, PADDED_RANK).astype(jnp.int32)
    initial_left_basis = centred(arg_keys[3], (MODEL_WIDTH, K), MODEL_WIDTH ** -0.5, 0.09375, ((0, 16),), jnp.float32)
    initial_right_basis = centred(arg_keys[4], (MODEL_WIDTH, K), MODEL_WIDTH ** -0.5, 0.09375, ((0, 16),), jnp.float32)
    return {"up_factors_wide": up_factors_wide, "transposed_down_factors": transposed_down_factors, "ranks": ranks, "initial_left_basis": initial_left_basis, "initial_right_basis": initial_right_basis}


def column_scale(ranks):
    positions = jnp.arange(PADDED_RANK, dtype=jnp.int32)
    live = positions[None, :] < ranks[:, None]
    factor = 4.0 / jnp.sqrt(ranks.astype(jnp.float32))
    return jnp.where(live, factor[:, None], jnp.float32(0.0)).reshape(-1).astype(jnp.float32)

def split_into_blocks(factors):
    width = factors.shape[1] // N_ADAPTER
    return factors.reshape(factors.shape[0], N_ADAPTER, width).transpose(1, 0, 2)

def project_all(basis, blocks, column_scaling):

    def one_block(block):
        return jnp.dot(basis.T, block.astype(jnp.float32), precision=lax.Precision.HIGHEST)
    pieces = lax.map(one_block, blocks)
    return pieces.transpose(1, 0, 2).reshape(basis.shape[1], -1) * column_scaling[None, :]

def coupling_of(own_proj, other_proj, column_scaling):
    count = own_proj.shape[1] // PADDED_RANK
    own_rows = own_proj.reshape(own_proj.shape[0], count, PADDED_RANK)
    other_rows = other_proj.reshape(other_proj.shape[0], count, PADDED_RANK)
    gram_small = jnp.einsum('kar,kas->ars', other_rows, other_rows, precision=lax.Precision.HIGHEST)
    coupling = jnp.einsum('ars,kas->ark', gram_small, own_rows, precision=lax.Precision.HIGHEST)
    return coupling.reshape(count * PADDED_RANK, own_proj.shape[0]) * column_scaling[:, None]

def combine_update(blocks, coupling):
    width = blocks.shape[2]
    pieces = coupling.reshape(N_ADAPTER, width, coupling.shape[1])

    def step_fn(total, pair):
        block, piece = pair
        return (total + jnp.dot(block.astype(jnp.float32), piece, precision=lax.Precision.HIGHEST), None)
    start_total = jnp.zeros((blocks.shape[1], coupling.shape[1]), jnp.float32)
    total, unused = lax.scan(step_fn, start_total, (blocks, pieces))
    return total

def cholesky_basis(update):
    gram_sum = jnp.dot(update.T, update, precision=lax.Precision.HIGHEST)
    lower = jnp.linalg.cholesky(gram_sum)
    return lax.linalg.triangular_solve(lower, update, left_side=False, lower=True, transpose_a=True)

def reference(up_factors_wide, transposed_down_factors, ranks, initial_left_basis, initial_right_basis):
    column_scaling = column_scale(ranks)
    up_factor_blocks = split_into_blocks(up_factors_wide)
    down_factor_blocks = split_into_blocks(transposed_down_factors)
    left_projected = project_all(initial_left_basis, up_factor_blocks, column_scaling)
    right_projected = project_all(initial_right_basis, down_factor_blocks, column_scaling)
    for sweep_index in range(ITERS):
        update = combine_update(up_factor_blocks, coupling_of(left_projected, right_projected, column_scaling))
        initial_left_basis = cholesky_basis(update)
        left_projected = project_all(initial_left_basis, up_factor_blocks, column_scaling)
        update = combine_update(down_factor_blocks, coupling_of(right_projected, left_projected, column_scaling))
        initial_right_basis = cholesky_basis(update)
        right_projected = project_all(initial_right_basis, down_factor_blocks, column_scaling)
    count = left_projected.shape[1] // PADDED_RANK
    p_rows = left_projected.reshape(K, count, PADDED_RANK)
    q_rows = right_projected.reshape(K, count, PADDED_RANK)
    cores = jnp.einsum('kar,jar->akj', p_rows, q_rows, precision=lax.Precision.HIGHEST)
    return (initial_left_basis, initial_right_basis, cores)
```

```python
import functools

import jax
import jax.numpy as jnp
from jax import lax
from jax.experimental import pallas as pl
from jax.experimental.pallas import tpu as pltpu
from jax.sharding import PartitionSpec as P

PADDED_RANK = 16
ITERS = 2
RING = 4
K = 256
PANEL = 32
HIGH = lax.Precision.HIGHEST
F32 = jnp.float32
BF16 = jnp.bfloat16
VMEM = pl.BlockSpec(memory_space=pltpu.VMEM)
SMEM = pl.BlockSpec(memory_space=pltpu.SMEM)
PARAMS = pltpu.CompilerParams(vmem_limit_bytes=32 * 1024 * 1024)


def call(kernel, outs, n_in, flops, nbytes, scratch=(), smem=0):
    return pl.pallas_call(
        kernel,
        out_shape=outs,
        in_specs=[SMEM] * smem + [VMEM] * (n_in - smem),
        out_specs=jax.tree.map(lambda _: VMEM, outs),
        scratch_shapes=list(scratch),
        compiler_params=PARAMS,
        cost_estimate=pl.CostEstimate(flops=flops, bytes_accessed=nbytes, transcendentals=0),
    )


def f32s(*shape):
    return jax.ShapeDtypeStruct(shape, F32)


def shift(axis, d):
    if axis == "x":
        return "adapter", [(i, ((i // 2 + d) % RING) * 2 + i % 2) for i in range(8)]
    if axis == "core":
        return "adapter", [(i, i ^ 1) for i in range(8)]
    if axis == "y":
        return "row", [(i, (i // 4) * 4 + (i % 4 + d) % RING) for i in range(16)]
    return "row", [(i, ((i // 4 + d) % RING) * 4 + i % 4) for i in range(16)]


def send(value, axis, d=1):
    name, perm = shift(axis, d)
    return lax.ppermute(value, name, perm)


def exchange(value, axis):
    return [value] + [send(value, axis, d) for d in (1, 2, 3)]


def split3(value):
    high = value.astype(BF16)
    rest = value - high.astype(F32)
    mid = rest.astype(BF16)
    return high, mid, (rest - mid.astype(F32)).astype(BF16)


def arrange_kernel(pos_ref, a_ref, o_ref):
    c, z, y = pos_ref[1], pos_ref[2], pos_ref[3]
    for h in range(2):
        for first in range(RING):
            for second in range(RING):
                dy, dz = (first, second) if h == 0 else (second, first)
                source = lax.rem(z + RING - dz, RING) * RING + lax.rem(y + RING - dy, RING)
                block = a_ref[source, h]
                swapped = jnp.concatenate([block[:, 128:], block[:, :128]], axis=1)
                at = (h * 16 + first * 4 + second) * 96
                o_ref[at : at + 96, :] = jnp.where(c == 0, block, swapped)


def arrange(pos, factors):
    turned = factors.T.reshape(16, 2, 96, 256)
    return call(
        arrange_kernel, jax.ShapeDtypeStruct((3072, 256), BF16), 2, 0, 3 << 20, smem=1
    )(pos, turned)


def project_kernel(a_ref, top_ref, low_ref, *o_refs):
    parts = split3(jnp.concatenate([top_ref[...], low_ref[...]], axis=0))
    for i, o_ref in enumerate(o_refs):
        block = a_ref[i * 384 : (i + 1) * 384, :]
        o_ref[...] = sum(
            jnp.dot(block, part, preferred_element_type=F32) for part in reversed(parts)
        )


def project(turned, top, low):
    return call(project_kernel, [f32s(384, 256)] * 8, 3, 6 * 3072 << 16, 5 << 20)(
        turned, top, low
    )


def gram_kernel(pos_ref, top_ref, low_ref, o_ref, g_ref):
    g = sum(
        lax.dot_general(r[...], r[...], (((0,), (0,)), ((), ())), precision=HIGH,
                        preferred_element_type=F32)
        for r in (top_ref, low_ref)
    )
    g_ref[...] = g
    at = pl.multiple_of((pos_ref[0] * 2 + pos_ref[1]) * 32, 32)
    o_ref[...] = g_ref[pl.ds(at, 32), :]


def gram(pos, top, low):
    return call(gram_kernel, f32s(32, 256), 3, 12 << 24, 1 << 19,
                [pltpu.VMEM((256, 256), F32)], smem=1)(pos, top, low)


def inverse_kernel(pos_ref, g0, g1, g2, g3, o_ref, w_ref):
    x = pos_ref[0]
    for dx, g in enumerate((g0, g1, g2, g3)):
        at = pl.multiple_of(lax.rem(x + RING - dx, RING) * 64, 64)
        w_ref[pl.ds(at, 64), :] = g[...]
    lane = lax.broadcasted_iota(jnp.int32, (PANEL, K), 1)
    row = lax.broadcasted_iota(jnp.int32, (PANEL, K), 0)
    row_one = lax.broadcasted_iota(jnp.int32, (PANEL, 1), 0)
    lane_one = lax.broadcasted_iota(jnp.int32, (1, K), 1)
    all_lane = lax.broadcasted_iota(jnp.int32, (K, K), 1)
    all_row = lax.broadcasted_iota(jnp.int32, (K, K), 0)
    for lo in range(0, K, PANEL):
        hi = lo + PANEL
        r = w_ref[lo:hi, :]
        pivots = jnp.ones((PANEL, 1), F32)
        for j in range(PANEL):
            at = lo + j
            pivot = r[j : j + 1, at : at + 1]
            column = jnp.where(row_one > j, r[:, at : at + 1], 0.0)
            line = jnp.where(lane_one == at, 1.0, r[j : j + 1, :]) * (1.0 / pivot)
            pivots = jnp.where(row_one == j, pivot, pivots)
            kept = jnp.where((lane == at) & (row >= j), jnp.where(row == j, 1.0, 0.0), r)
            r = kept - column * line
        clean = jnp.where((lane < hi) & (lane > row + lo), 0.0, r)
        o_ref[lo:hi, :] = jnp.where(lane <= row + lo, clean, 0.0) * lax.rsqrt(pivots)
        if hi < K:
            times = jnp.where(lane >= hi, r, 0.0) / pivots
            change = jnp.dot(times.T, clean, precision=HIGH, preferred_element_type=F32)
            gone = (all_lane >= lo) & (all_lane < hi) & (all_row >= hi)
            w_ref[...] = jnp.where(gone, 0.0, w_ref[...]) - change


def inverse_factor(pos, pieces):
    return call(inverse_kernel, f32s(K, K), 5, 1 << 31, 1 << 19,
                [pltpu.VMEM((K, K), F32)], smem=1)(pos, *pieces)


def block_mask(n):
    rows = lax.broadcasted_iota(jnp.int32, (n, n), 0) // PADDED_RANK
    return rows == lax.broadcasted_iota(jnp.int32, (n, n), 1) // PADDED_RANK


def couple(own, other, scale):
    small = lax.dot_general(other, other, (((1,), (1,)), ((), ())), precision=HIGH,
                            preferred_element_type=F32)
    small = jnp.where(block_mask(192), small, 0.0)
    return jnp.dot(small, own, precision=HIGH, preferred_element_type=F32) * scale


def first_kernel(*refs):
    left, right = refs[0:8], refs[8:16]
    scale_ref, c0, c1, p_ref, q_ref = refs[16:]
    scale = scale_ref[...]
    p, q = (
        jnp.concatenate([sum(r[...] for r in s[0:4]), sum(r[...] for r in s[4:8])], axis=0) * scale
        for s in (left, right)
    )
    coupling = couple(p, q, scale)
    c0[...] = coupling[:96]
    c1[...] = coupling[96:]
    p_ref[...] = p
    q_ref[...] = q


def next_kernel(*refs):
    pieces = refs[0:8]
    linv_ref, scale_ref, other_ref, c0, c1, p_ref = refs[8:]
    scale = scale_ref[...]
    total = jnp.concatenate(
        [sum(r[...] for r in pieces[0:4]), sum(r[...] for r in pieces[4:8])], axis=0
    )
    p = lax.dot_general(total, linv_ref[...], (((1,), (1,)), ((), ())), precision=HIGH,
                        preferred_element_type=F32) * scale
    coupling = couple(other_ref[...], p, scale)
    c0[...] = coupling[:96]
    c1[...] = coupling[96:]
    p_ref[...] = p


def last_kernel(*refs):
    pieces = refs[0:8]
    linv_ref, scale_ref, q0, q1 = refs[8:]
    total = jnp.concatenate(
        [sum(r[...] for r in pieces[0:4]), sum(r[...] for r in pieces[4:8])], axis=0
    )
    q = lax.dot_general(total, linv_ref[...], (((1,), (1,)), ((), ())), precision=HIGH,
                        preferred_element_type=F32) * scale_ref[...]
    q0[...] = q[:96]
    q1[...] = q[96:]


def update_kernel(a_ref, *refs):
    blocks, (keep_ref, send_ref) = refs[:8], refs[8:]
    total = jnp.zeros((256, 256), F32)
    for i, block in enumerate(blocks):
        a = a_ref[:, i * 384 : (i + 1) * 384]
        total += sum(
            jnp.dot(a, part, preferred_element_type=F32) for part in reversed(split3(block[...]))
        )
    keep_ref[...] = total[:128]
    send_ref[...] = total[128:]


def update(factors, blocks):
    return call(update_kernel, [f32s(128, 256)] * 2, 9, 6 * 3072 << 16, 5 << 20)(
        factors, *blocks
    )


def basis_kernel(pos_ref, top_ref, low_ref, linv_ref, o_ref):
    c = pos_ref[1]
    linv = linv_ref[...]
    for at, r in ((c, top_ref), (1 - c, low_ref)):
        o_ref[pl.ds(pl.multiple_of(at * 128, 128), 128), :] = lax.dot_general(
            r[...], linv, (((1,), (1,)), ((), ())), precision=HIGH, preferred_element_type=F32
        )


def basis_of(pos, top, low, linv):
    return call(basis_kernel, f32s(256, 256), 4, 12 << 24, 1 << 20, smem=1)(
        pos, top, low, linv
    )


def cores_kernel(pos_ref, p_ref, *refs):
    blocks, o_ref = refs[:8], refs[8]
    z, y = pos_ref[2], pos_ref[3]
    mask = block_mask(96)
    for h in range(2):
        for first in range(RING):
            for second in range(RING):
                dy, dz = (first, second) if h == 0 else (second, first)
                source = lax.rem(z + RING - dz, RING) * RING + lax.rem(y + RING - dy, RING)
                p = p_ref[source, h]
                wide = jnp.where(mask, jnp.concatenate([p] * 6, axis=0), 0.0)
                q = blocks[h * 4 + first][second * 96 : second * 96 + 96, :]
                core = jnp.dot(wide, q, precision=HIGH, preferred_element_type=F32)
                o_ref[pl.ds(source * 12 + h * 6, 6)] = core.reshape(6, 16, 256)


def scatter(blocks):
    pieces = []
    for mine, (axis, other) in ((blocks[:4], ("y", "z")), (blocks[4:], ("z", "y"))):
        arrived = [mine[0]] + [send(mine[d], axis, -d) for d in (1, 2, 3)]
        parts = [sum(a[i * 96 : i * 96 + 96] for a in arrived) for i in range(RING)]
        pieces += [parts[0]] + [send(parts[d], other, -d) for d in (1, 2, 3)]
    return pieces


def gather(halves):
    blocks = []
    for half, (axis, other) in zip(halves, (("z", "y"), ("y", "z"))):
        blocks += exchange(jnp.concatenate(exchange(half, axis), axis=0), other)
    return blocks


def refit(pos, factors, turned, coupling):
    keep, other = update(factors, gather(coupling))
    half = sum(exchange(keep + send(other, "core"), "x"))
    rest = send(half, "core")
    piece = gram(pos, half, rest)
    piece = sum(exchange(piece, "z"))
    piece = sum(exchange(piece, "y"))
    mate = send(piece, "core")
    pair = jnp.where(
        pos[1] == 0,
        jnp.concatenate([piece, mate], axis=0),
        jnp.concatenate([mate, piece], axis=0),
    )
    linv = inverse_factor(pos, exchange(pair, "x"))
    pieces = scatter(project(turned, half, rest))
    return half, rest, linv, pieces


def column_scale(ranks):
    positions = jnp.arange(PADDED_RANK, dtype=jnp.int32)
    live = positions[None, :] < ranks[:, None]
    factor = 4.0 / jnp.sqrt(ranks.astype(F32))
    return jnp.where(live, factor[:, None], F32(0.0)).reshape(-1, 1)


def shards(up, down, ranks, left, right):
    adapter, row = lax.axis_index("adapter"), lax.axis_index("row")
    c = adapter % 2
    pos = jnp.stack([adapter // 2, c, row // 4, row % 4]).astype(jnp.int32)
    scale = column_scale(lax.dynamic_slice_in_dim(ranks, row * 12, 12, 0))

    def halves(basis):
        return (
            lax.dynamic_slice_in_dim(basis, c * 128, 128, 0),
            lax.dynamic_slice_in_dim(basis, (1 - c) * 128, 128, 0),
        )

    up_turned = arrange(pos, up)
    left_pieces = scatter(project(up_turned, *halves(left)))
    down_turned = arrange(pos, down)
    right_pieces = scatter(project(down_turned, *halves(right)))
    up, down = up_turned.T, down_turned.T
    c0, c1, p, q = call(
        first_kernel, [f32s(96, 256)] * 2 + [f32s(192, 256)] * 2, 17, 1 << 28, 3 << 20
    )(*left_pieces, *right_pieces, scale)

    step = call(next_kernel, [f32s(96, 256)] * 2 + [f32s(192, 256)], 11, 1 << 29, 3 << 20)
    for sweep in range(ITERS):
        top, low, linv, pieces = refit(pos, up, up_turned, (c0, c1))
        if sweep == ITERS - 1:
            left = basis_of(pos, top, low, linv)
        c0, c1, p = step(*pieces, linv, scale, q)
        if sweep == ITERS - 1:
            sent = p.reshape(2, 96, 16, 16).transpose(2, 0, 3, 1)
            p_rows = lax.all_to_all(sent, "row", 0, 0)
        top, low, linv, pieces = refit(pos, down, down_turned, (c0, c1))
        if sweep == ITERS - 1:
            right = basis_of(pos, top, low, linv)
            q_halves = call(last_kernel, [f32s(96, 256)] * 2, 10, 1 << 28, 2 << 20)(
                *pieces, linv, scale
            )
        else:
            c0, c1, q = step(*pieces, linv, scale, p)
    cores = call(cores_kernel, f32s(192, 16, 256), 10, 1 << 30, 6 << 20, smem=1)(
        pos, p_rows, *gather(q_halves)
    )
    return left, right, cores


def solution(mesh):
    return jax.shard_map(
        shards,
        mesh=mesh,
        in_specs=(
            P("row", "adapter"),
            P("row", "adapter"),
            P("adapter"),
            P("row", None),
            P("row", None),
        ),
        out_specs=(P("row", None), P("row", None), P("adapter", "row", None)),
        check_vma=False,
    )
```

```python
import jax
import jax.numpy as jnp
from jax import lax
from jax.experimental import pallas as pl
from jax.experimental.pallas import tpu as pltpu
from jax.sharding import PartitionSpec as P

PADDED_RANK = 16
ITERS = 2
RING = 4
K = 256
PANEL = 32
ORDER = (0, 1, 3, 2)
HIGH = lax.Precision.HIGHEST
F32 = jnp.float32
BF16 = jnp.bfloat16
VMEM = pl.BlockSpec(memory_space=pltpu.VMEM)
SMEM = pl.BlockSpec(memory_space=pltpu.SMEM)
PARAMS = pltpu.CompilerParams(vmem_limit_bytes=32 * 1024 * 1024)


def call(kernel, outs, n_in, flops, nbytes, scratch=(), smem=0):
    return pl.pallas_call(
        kernel,
        out_shape=outs,
        in_specs=[SMEM] * smem + [VMEM] * (n_in - smem),
        out_specs=jax.tree.map(lambda _: VMEM, outs),
        scratch_shapes=list(scratch),
        compiler_params=PARAMS,
        cost_estimate=pl.CostEstimate(flops=flops, bytes_accessed=nbytes, transcendentals=0),
    )


def f32s(*shape):
    return jax.ShapeDtypeStruct(shape, F32)


def moved(axis, d, x, c, z, y):
    if axis == "core":
        return x, 1 - c, z, y
    if axis == "x":
        return (x + d) % RING, c, z, y
    if (axis == "first") == (c == 0):
        return x, c, z, (y + d) % RING
    return x, c, (z + d) % RING, y


def send(value, axis, d=1):
    perm = []
    for i in range(128):
        x, c, z, y = moved(axis, d, i // 32, i // 16 % 2, i // 4 % 4, i % 4)
        perm.append((i, x * 32 + c * 16 + z * 4 + y))
    return lax.ppermute(value, ("adapter", "row"), perm)


def exchange(value, axis):
    return [value] + [send(value, axis, d) for d in (1, 3, 2)]


def chunk_at(pos_ref, first, second):
    c, z, y = pos_ref[1], pos_ref[2], pos_ref[3]
    dy = jnp.where(c == 0, first, second)
    dz = jnp.where(c == 0, second, first)
    return lax.rem(z + RING - dz, RING) * RING + lax.rem(y + RING - dy, RING)


def split3(value):
    high = value.astype(BF16)
    rest = value - high.astype(F32)
    mid = rest.astype(BF16)
    return high, mid, (rest - mid.astype(F32)).astype(BF16)


def arrange_kernel(pos_ref, a_ref, o_ref):
    for i, first in enumerate(ORDER):
        for j, second in enumerate(ORDER):
            block = a_ref[chunk_at(pos_ref, first, second)]
            swapped = jnp.concatenate([block[:, 128:], block[:, :128]], axis=1)
            at = (i * 4 + j) * 192
            o_ref[at : at + 192, :] = jnp.where(pos_ref[1] == 0, block, swapped)


def arrange(pos, factors):
    return call(
        arrange_kernel, jax.ShapeDtypeStruct((3072, 256), BF16), 2, 0, 3 << 20, smem=1
    )(pos, factors.T.reshape(16, 192, 256))


def project_kernel(a_ref, top_ref, low_ref, *o_refs):
    parts = split3(jnp.concatenate([top_ref[...], low_ref[...]], axis=0))
    for i, o_ref in enumerate(o_refs):
        block = a_ref[i * 768 : (i + 1) * 768, :]
        o_ref[...] = sum(
            jnp.dot(block, part, preferred_element_type=F32) for part in reversed(parts)
        )


def project(turned, top, low):
    return call(project_kernel, [f32s(768, 256)] * 4, 3, 6 * 3072 << 16, 5 << 20)(
        turned, top, low
    )


def gram_kernel(pos_ref, top_ref, low_ref, o_ref, g_ref):
    g_ref[...] = sum(
        lax.dot_general(r[...], r[...], (((0,), (0,)), ((), ())), precision=HIGH,
                        preferred_element_type=F32)
        for r in (top_ref, low_ref)
    )
    o_ref[...] = g_ref[pl.ds(pl.multiple_of(pos_ref[1] * 128, 128), 128), :]


def gram(pos, top, low):
    return call(gram_kernel, f32s(128, 256), 3, 12 << 24, 1 << 19,
                [pltpu.VMEM((256, 256), F32)], smem=1)(pos, top, low)


def eliminate(tall, at):
    n = tall.shape[0]
    sub = lax.broadcasted_iota(jnp.int32, (n, 128), 0)
    lane = lax.broadcasted_iota(jnp.int32, (n, 128), 1)
    half, base = at // 128, at % 128
    columns = [
        jnp.broadcast_to(tall[:, at + k : at + k + 1], (n, 128)) for k in range(8)
    ]
    sides = [tall[:, :128], tall[:, 128:]]
    pivots = jnp.ones((8, 128), F32)
    for j in range(8):
        pivot = columns[j][j : j + 1, :]
        times = jnp.where(sub > j, columns[j], 0.0) * (1.0 / pivot)
        pivots = jnp.where(sub[:8] == j, pivot, pivots)
        for k in range(j + 1, 8):
            columns[k] = columns[k] - times * columns[k][j : j + 1, :]
        here = lane == base + j
        kept = jnp.where(here & (sub >= j), jnp.where(sub == j, 1.0, 0.0), sides[half])
        other = sides[1 - half]
        sides[half] = kept - times * kept[j : j + 1, :]
        sides[1 - half] = other - times * other[j : j + 1, :]
    return jnp.concatenate(sides, axis=1), pivots


def inverse_kernel(pos_ref, mine_ref, mate_ref, o_ref, w_ref):
    for c, ref in ((pos_ref[1], mine_ref), (1 - pos_ref[1], mate_ref)):
        w_ref[pl.ds(pl.multiple_of(c * 128, 128), 128), :] = ref[...]
    lane = lax.broadcasted_iota(jnp.int32, (PANEL, K), 1)
    row = lax.broadcasted_iota(jnp.int32, (PANEL, K), 0)
    all_lane = lax.broadcasted_iota(jnp.int32, (K, K), 1)
    all_row = lax.broadcasted_iota(jnp.int32, (K, K), 0)
    for lo in range(0, K, PANEL):
        hi = lo + PANEL
        rest = w_ref[lo:hi, :]
        done, pivots = [], []
        for at in range(lo, hi, 8):
            rest, found = eliminate(rest, at)
            done.append(rest[:8])
            pivots.append(found)
            rest = rest[8:]
        r = jnp.concatenate(done, axis=0)
        pivots = jnp.concatenate(pivots, axis=0)
        pivots = jnp.concatenate([pivots, pivots], axis=1)
        clean = jnp.where((lane < hi) & (lane > row + lo), 0.0, r)
        o_ref[lo:hi, :] = jnp.where(lane <= row + lo, clean, 0.0) * lax.rsqrt(pivots)
        if hi < K:
            times = jnp.where(lane >= hi, r, 0.0) / pivots
            change = jnp.dot(times.T, clean, precision=HIGH, preferred_element_type=F32)
            gone = (all_lane >= lo) & (all_lane < hi) & (all_row >= hi)
            w_ref[...] = jnp.where(gone, 0.0, w_ref[...]) - change


def inverse_factor(pos, mine, mate):
    return call(inverse_kernel, f32s(K, K), 3, 1 << 33, 1 << 19,
                [pltpu.VMEM((K, K), F32)], smem=1)(pos, mine, mate)


def block_mask(n):
    rows = lax.broadcasted_iota(jnp.int32, (n, n), 0) // PADDED_RANK
    return rows == lax.broadcasted_iota(jnp.int32, (n, n), 1) // PADDED_RANK


def couple(own, other, scale):
    small = lax.dot_general(other, other, (((1,), (1,)), ((), ())), precision=HIGH,
                            preferred_element_type=F32)
    small = jnp.where(block_mask(192), small, 0.0)
    return jnp.dot(small, own, precision=HIGH, preferred_element_type=F32) * scale


def first_kernel(*refs):
    left, right = refs[0:4], refs[4:8]
    scale_ref, c_ref, p_ref, q_ref = refs[8:]
    scale = scale_ref[...]
    p, q = (sum(r[...] for r in side) * scale for side in (left, right))
    c_ref[...] = couple(p, q, scale)
    p_ref[...] = p
    q_ref[...] = q


def normalised(pieces, linv_ref, scale):
    return lax.dot_general(sum(r[...] for r in pieces), linv_ref[...], (((1,), (1,)), ((), ())),
                           precision=HIGH, preferred_element_type=F32) * scale


def next_kernel(*refs):
    linv_ref, scale_ref, other_ref, c_ref, p_ref = refs[4:]
    scale = scale_ref[...]
    p = normalised(refs[:4], linv_ref, scale)
    c_ref[...] = couple(other_ref[...], p, scale)
    p_ref[...] = p


def last_kernel(*refs):
    linv_ref, scale_ref, q_ref = refs[4:]
    q_ref[...] = normalised(refs[:4], linv_ref, scale_ref[...])


def product(a_ref, places, blocks):
    total = 0.0
    for i, block in zip(places, blocks):
        a = a_ref[:, i * 768 : (i + 1) * 768]
        total += sum(
            jnp.dot(a, part, preferred_element_type=F32) for part in reversed(split3(block[...]))
        )
    return total


def early_kernel(a_ref, b0, b1, b2, o_ref):
    o_ref[...] = product(a_ref, (0, 1, 2), (b0, b1, b2))


def late_kernel(a_ref, b3, part_ref, keep_ref, send_ref):
    total = part_ref[...] + product(a_ref, (3,), (b3,))
    keep_ref[...] = total[:128]
    send_ref[...] = total[128:]


def update(factors, blocks):
    part = call(early_kernel, f32s(256, 256), 4, 4 * 3072 << 16, 4 << 20)(factors, *blocks[:3])
    return call(late_kernel, [f32s(128, 256)] * 2, 3, 3 * 3072 << 16, 2 << 20)(
        factors, blocks[3], part
    )


def basis_kernel(pos_ref, top_ref, low_ref, linv_ref, o_ref):
    c = pos_ref[1]
    linv = linv_ref[...]
    for at, r in ((c, top_ref), (1 - c, low_ref)):
        o_ref[pl.ds(pl.multiple_of(at * 128, 128), 128), :] = lax.dot_general(
            r[...], linv, (((1,), (1,)), ((), ())), precision=HIGH, preferred_element_type=F32
        )


def basis_of(pos, top, low, linv):
    return call(basis_kernel, f32s(256, 256), 4, 12 << 24, 1 << 20, smem=1)(
        pos, top, low, linv
    )


def cores_kernel(pos_ref, p_ref, *refs):
    blocks, o_ref = refs[:4], refs[4]
    mask = block_mask(192)
    for i, first in enumerate(ORDER):
        for j, second in enumerate(ORDER):
            source = chunk_at(pos_ref, first, second)
            wide = jnp.where(mask, jnp.concatenate([p_ref[source]] * 12, axis=0), 0.0)
            q = blocks[i][j * 192 : j * 192 + 192, :]
            core = jnp.dot(wide, q, precision=HIGH, preferred_element_type=F32)
            o_ref[pl.ds(source * 12, 12)] = core.reshape(12, 16, 256)


def join_kernel(b0, b1, b2, b3, o_ref):
    for i, b in enumerate((b0, b1, b2, b3)):
        o_ref[i * 192 : (i + 1) * 192, :] = b[...]


def scatter_start(blocks):
    return [blocks[0]] + [send(b, "first", -d) for d, b in zip(ORDER[1:], blocks[1:])]


def scatter_end(arrived):
    parts = [sum(a[i * 192 : i * 192 + 192] for a in arrived) for i in range(RING)]
    return [parts[0]] + [send(p, "second", -d) for d, p in zip(ORDER[1:], parts[1:])]


def gather(value):
    joined = call(join_kernel, f32s(768, 256), 4, 0, 2 << 20)(*exchange(value, "second"))
    return exchange(joined, "first")


def refit(pos, factors, turned, coupling):
    keep, other = update(factors, gather(coupling))
    half = sum(exchange(keep + send(other, "core"), "x"))
    rest = send(half, "core")
    piece = gram(pos, half, rest)
    piece = sum(exchange(piece, "first"))
    arrived = scatter_start(project(turned, half, rest))
    piece = sum(exchange(piece, "second"))
    linv = inverse_factor(pos, piece, send(piece, "core"))
    linv, *arrived = lax.optimization_barrier((linv, *arrived))
    return half, rest, linv, scatter_end(arrived)


def column_scale(ranks):
    positions = jnp.arange(PADDED_RANK, dtype=jnp.int32)
    live = positions[None, :] < ranks[:, None]
    factor = 4.0 / jnp.sqrt(ranks.astype(F32))
    return jnp.where(live, factor[:, None], F32(0.0)).reshape(-1, 1)


def shards(up, down, ranks, left, right):
    adapter, row = lax.axis_index("adapter"), lax.axis_index("row")
    c = adapter % 2
    pos = jnp.stack([adapter // 2, c, row // 4, row % 4]).astype(jnp.int32)
    scale = column_scale(lax.dynamic_slice_in_dim(ranks, row * 12, 12, 0))

    def halves(basis):
        return (
            lax.dynamic_slice_in_dim(basis, c * 128, 128, 0),
            lax.dynamic_slice_in_dim(basis, (1 - c) * 128, 128, 0),
        )

    up_turned = arrange(pos, up)
    left_pieces = scatter_start(project(up_turned, *halves(left)))
    down_turned = arrange(pos, down)
    right_pieces = scatter_start(project(down_turned, *halves(right)))
    left_pieces, right_pieces = scatter_end(left_pieces), scatter_end(right_pieces)
    up, down = up_turned.T, down_turned.T
    side = f32s(192, 256)
    coupling, p, q = call(first_kernel, [side] * 3, 9, 1 << 28, 3 << 20)(
        *left_pieces, *right_pieces, scale
    )

    step = call(next_kernel, [side] * 2, 7, 1 << 29, 3 << 20)
    for sweep in range(ITERS):
        top, low, linv, pieces = refit(pos, up, up_turned, coupling)
        if sweep == ITERS - 1:
            left = basis_of(pos, top, low, linv)
        coupling, p = step(*pieces, linv, scale, q)
        if sweep == ITERS - 1:
            p_rows = lax.all_to_all(p.T.reshape(16, 16, 192), "row", 0, 0)
        top, low, linv, pieces = refit(pos, down, down_turned, coupling)
        if sweep == ITERS - 1:
            right = basis_of(pos, top, low, linv)
            q = call(last_kernel, side, 6, 1 << 28, 2 << 20)(*pieces, linv, scale)
        else:
            coupling, q = step(*pieces, linv, scale, p)
    cores = call(cores_kernel, f32s(192, 16, 256), 6, 1 << 30, 6 << 20, smem=1)(
        pos, p_rows, *gather(q)
    )
    return left, right, cores


def solution(mesh):
    return jax.shard_map(
        shards,
        mesh=mesh,
        in_specs=(
            P("row", "adapter"),
            P("row", "adapter"),
            P("adapter"),
            P("row", None),
            P("row", None),
        ),
        out_specs=(P("row", None), P("row", None), P("adapter", "row", None)),
        check_vma=False,
    )
```

```python
import functools

import jax
import jax.numpy as jnp
from jax import lax
from jax.experimental import pallas as pl
from jax.experimental.pallas import tpu as pltpu
from jax.sharding import PartitionSpec as P

PADDED_RANK = 16
ITERS = 2
RING = 4
K = 256
PANEL = 32
ORDER = (0, 1, 3, 2)
HIGH = lax.Precision.HIGHEST
F32 = jnp.float32
BF16 = jnp.bfloat16
VMEM = pl.BlockSpec(memory_space=pltpu.VMEM)
SMEM = pl.BlockSpec(memory_space=pltpu.SMEM)
PARAMS = pltpu.CompilerParams(vmem_limit_bytes=20 * 1024 * 1024)


def call(kernel, outs, n_in, flops, nbytes, scratch=(), smem=0):
    return pl.pallas_call(
        kernel,
        out_shape=outs,
        in_specs=[SMEM] * smem + [VMEM] * (n_in - smem),
        out_specs=jax.tree.map(lambda _: VMEM, outs),
        scratch_shapes=list(scratch),
        compiler_params=PARAMS,
        cost_estimate=pl.CostEstimate(flops=flops, bytes_accessed=nbytes, transcendentals=0),
    )


def f32s(*shape):
    return jax.ShapeDtypeStruct(shape, F32)


def moved(axis, d, x, c, z, y):
    if axis == "core":
        return x, 1 - c, z, y
    if axis[c] == "x":
        return (x + d) % RING, c, z, y
    if axis[c] == "y":
        return x, c, z, (y + d) % RING
    return x, c, (z + d) % RING, y


def send(value, axis, d=1):
    perm = []
    for i in range(128):
        x, c, z, y = moved(axis, d, i // 32, i // 16 % 2, i // 4 % 4, i % 4)
        perm.append((i, x * 32 + c * 16 + z * 4 + y))
    return lax.ppermute(value, ("adapter", "row"), perm)


def exchange(value, axis):
    return [value] + [send(value, axis, d) for d in ORDER[1:]]


def deliver(values, axis, sign=-1):
    return [values[0]] + [send(v, axis, sign * d) for d, v in zip(ORDER[1:], values[1:])]


def back(place, d):
    return lax.rem(place + RING - d, RING)


def chunk_at(pos_ref, first, second):
    c, z, y = pos_ref[1], pos_ref[2], pos_ref[3]
    dy = jnp.where(c == 0, first, second)
    dz = jnp.where(c == 0, second, first)
    return back(z, dz) * RING + back(y, dy)


LEFT, RIGHT = "y", "z"
PLACE = {"z": 2, "y": 3}
CROSS = {"y": "z", "z": "y"}


def block_place(pos_ref, place):
    return lax.bitwise_xor(place // 2, pos_ref[1]) * 2 + lax.rem(place, 2)


def split3(value):
    high = value.astype(BF16)
    rest = value - high.astype(F32)
    mid = rest.astype(BF16)
    return high, mid, (rest - mid.astype(F32)).astype(BF16)


def pieces_kernel(side, pos_ref, a_ref, *o_refs):
    at, cross = pos_ref[PLACE[side]], pos_ref[PLACE[CROSS[side]]]
    for o_ref, d in zip(o_refs, ORDER):
        mine = lax.rem(at + d, RING)
        for j, e in enumerate(ORDER):
            theirs = back(cross, e)
            source = theirs * RING + mine if side == "y" else mine * RING + theirs
            o_ref[j * 192 : j * 192 + 192, :] = a_ref[source].astype(F32)


def turned_kernel(side, pos_ref, *refs):
    for r, d in zip(refs[:-1], ORDER):
        refs[-1][block_place(pos_ref, back(pos_ref[PLACE[side]], d))] = r[...].astype(BF16)


def lay_out(side, pos, factors):
    pieces = call(functools.partial(pieces_kernel, side), [f32s(768, 256)] * 4, 2, 0, 5 << 20,
                  smem=1)(pos, factors.T.reshape(16, 192, 256))
    return call(functools.partial(turned_kernel, side), jax.ShapeDtypeStruct((4, 768, 256), BF16),
                5, 0, 5 << 20, smem=1)(pos, *deliver(pieces, side * 2, 1))


def spread_kernel(side, pos_ref, mine_ref, mate_ref, o_ref):
    for i, d in enumerate(ORDER):
        p = block_place(pos_ref, back(pos_ref[PLACE[side]], d))
        for c, ref in ((pos_ref[1], mine_ref), (1 - pos_ref[1], mate_ref)):
            at = pl.multiple_of(p * 256 + c * 128, 128)
            o_ref[pl.ds(at, 128), :] = ref[i * 128 : i * 128 + 128, :]


def spread(side, pos, basis):
    half = lax.dynamic_slice_in_dim(basis, pos[1] * 128, 128, 0)
    mine = jnp.concatenate(exchange(half, side * 2), axis=0)
    return call(functools.partial(spread_kernel, side), f32s(1024, 256), 3, 0, 2 << 20, smem=1)(
        pos, mine, send(mine, "core")
    )


def project_kernel(a_ref, *refs):
    sources, o_refs = refs[:-4], refs[-4:]
    parts = split3(jnp.concatenate([r[...] for r in sources], axis=0))
    for j, o_ref in enumerate(o_refs):
        block = jnp.concatenate([a_ref[p, j * 192 : j * 192 + 192, :] for p in range(4)], axis=1)
        o_ref[...] = sum(
            jnp.dot(block, part, preferred_element_type=F32) for part in reversed(parts)
        )


def project(turned, *sources):
    return call(project_kernel, [f32s(192, 256)] * 4, 1 + len(sources), 6 * 3072 << 16, 4 << 20)(
        turned, *sources
    )


def gram_kernel(pos_ref, top_ref, low_ref, o_ref, g_ref):
    g_ref[...] = sum(
        lax.dot_general(r[...], r[...], (((0,), (0,)), ((), ())), precision=HIGH,
                        preferred_element_type=F32)
        for r in (top_ref, low_ref)
    )
    o_ref[...] = g_ref[pl.ds(pl.multiple_of(pos_ref[1] * 128, 128), 128), :]


def gram(pos, top, low):
    return call(gram_kernel, f32s(128, 256), 3, 12 << 24, 1 << 19,
                [pltpu.VMEM((256, 256), F32)], smem=1)(pos, top, low)


def eliminate(tall, at):
    n = tall.shape[0]
    sub = lax.broadcasted_iota(jnp.int32, (n, 128), 0)
    lane = lax.broadcasted_iota(jnp.int32, (n, 128), 1)
    half, base = at // 128, at % 128
    columns = [
        jnp.broadcast_to(tall[:, at + k : at + k + 1], (n, 128)) for k in range(8)
    ]
    sides = [tall[:, :128], tall[:, 128:]]
    pivots = jnp.ones((8, 128), F32)
    for j in range(8):
        pivot = columns[j][j : j + 1, :]
        times = jnp.where(sub > j, columns[j], 0.0) * (1.0 / pivot)
        pivots = jnp.where(sub[:8] == j, pivot, pivots)
        for k in range(j + 1, 8):
            columns[k] = columns[k] - times * columns[k][j : j + 1, :]
        here = lane == base + j
        kept = jnp.where(here & (sub >= j), jnp.where(sub == j, 1.0, 0.0), sides[half])
        other = sides[1 - half]
        sides[half] = kept - times * kept[j : j + 1, :]
        sides[1 - half] = other - times * other[j : j + 1, :]
    return jnp.concatenate(sides, axis=1), pivots


def inverse_kernel(pos_ref, mine_ref, mate_ref, o_ref, w_ref):
    for c, ref in ((pos_ref[1], mine_ref), (1 - pos_ref[1], mate_ref)):
        w_ref[pl.ds(pl.multiple_of(c * 128, 128), 128), :] = ref[...]
    lane = lax.broadcasted_iota(jnp.int32, (PANEL, K), 1)
    row = lax.broadcasted_iota(jnp.int32, (PANEL, K), 0)
    all_lane = lax.broadcasted_iota(jnp.int32, (K, K), 1)
    all_row = lax.broadcasted_iota(jnp.int32, (K, K), 0)
    for lo in range(0, K, PANEL):
        hi = lo + PANEL
        rest = w_ref[lo:hi, :]
        done, pivots = [], []
        for at in range(lo, hi, 8):
            rest, found = eliminate(rest, at)
            done.append(rest[:8])
            pivots.append(found)
            rest = rest[8:]
        r = jnp.concatenate(done, axis=0)
        pivots = jnp.concatenate(pivots, axis=0)
        pivots = jnp.concatenate([pivots, pivots], axis=1)
        clean = jnp.where((lane < hi) & (lane > row + lo), 0.0, r)
        o_ref[lo:hi, :] = jnp.where(lane <= row + lo, clean, 0.0) * lax.rsqrt(pivots)
        if hi < K:
            times = jnp.where(lane >= hi, r, 0.0) / pivots
            change = jnp.dot(times.T, clean, precision=HIGH, preferred_element_type=F32)
            gone = (all_lane >= lo) & (all_lane < hi) & (all_row >= hi)
            w_ref[...] = jnp.where(gone, 0.0, w_ref[...]) - change


def inverse_factor(pos, mine, mate):
    return call(inverse_kernel, f32s(K, K), 3, 0, 1 << 10,
                [pltpu.VMEM((K, K), F32)], smem=1)(pos, mine, mate)


def block_mask(n):
    rows = lax.broadcasted_iota(jnp.int32, (n, n), 0) // PADDED_RANK
    return rows == lax.broadcasted_iota(jnp.int32, (n, n), 1) // PADDED_RANK


def couple(own, other, scale):
    small = lax.dot_general(other, other, (((1,), (1,)), ((), ())), precision=HIGH,
                            preferred_element_type=F32)
    small = jnp.where(block_mask(192), small, 0.0)
    return jnp.dot(small, own, precision=HIGH, preferred_element_type=F32) * scale


def first_kernel(*refs):
    left, right = refs[0:4], refs[4:8]
    scale_ref, c_ref, p_ref, q_ref = refs[8:]
    scale = scale_ref[...]
    p, q = (sum(r[...] for r in side) * scale for side in (left, right))
    c_ref[...] = couple(p, q, scale)
    p_ref[...] = p
    q_ref[...] = q


def normalised(pieces, linv_ref, scale):
    return lax.dot_general(sum(r[...] for r in pieces), linv_ref[...], (((1,), (1,)), ((), ())),
                           precision=HIGH, preferred_element_type=F32) * scale


def next_kernel(*refs):
    linv_ref, scale_ref, other_ref, c_ref, p_ref = refs[4:]
    scale = scale_ref[...]
    p = normalised(refs[:4], linv_ref, scale)
    c_ref[...] = couple(other_ref[...], p, scale)
    p_ref[...] = p


def last_kernel(*refs):
    linv_ref, scale_ref, q_ref = refs[4:]
    q_ref[...] = normalised(refs[:4], linv_ref, scale_ref[...])


def product(factors, blocks):
    return sum(
        jnp.dot(a[...], part, preferred_element_type=F32)
        for a, block in zip(factors, blocks)
        for part in reversed(split3(block[...]))
    )


def early_kernel(a0, a1, a2, b0, b1, b2, o_ref):
    o_ref[...] = product((a0, a1, a2), (b0, b1, b2))


def late_kernel(a3, b3, part_ref, keep_ref, send_ref):
    total = part_ref[...] + product((a3,), (b3,))
    keep_ref[...] = total[:512]
    send_ref[...] = total[512:]


def update(factors, blocks):
    part = call(early_kernel, f32s(1024, 256), 6, 4 * 3072 << 16, 3 << 20)(
        *factors[:3], *blocks[:3]
    )
    return call(late_kernel, [f32s(512, 256)] * 2, 3, 2 * 3072 << 16, 2 << 20)(
        factors[3], blocks[3], part
    )


def first_place(side, pos_ref):
    return jnp.where(pos_ref[1] == 0, pos_ref[0], pos_ref[PLACE[side]])


def split_kernel(side, pos_ref, keep_ref, other_ref, *o_refs):
    for o_ref, d in zip(o_refs, ORDER):
        at = pl.multiple_of(back(first_place(side, pos_ref), d) * 128, 128)
        o_ref[...] = keep_ref[pl.ds(at, 128), :] + other_ref[pl.ds(at, 128), :]


def merge_kernel(side, pos_ref, *refs):
    for r, d in zip(refs[:-1], ORDER):
        at = pl.multiple_of(back(first_place(side, pos_ref), d) * 128, 128)
        refs[-1][pl.ds(at, 128), :] = r[...]


def add_up(side, pos, keep, other):
    chunks = call(functools.partial(split_kernel, side), [f32s(128, 256)] * 4, 3, 0, 2 << 20,
                  smem=1)(pos, keep, send(other, "core"))
    chunk = sum(deliver(chunks, "x" + side))
    chunk = sum(exchange(chunk, side + "x"))
    return call(functools.partial(merge_kernel, side), f32s(512, 256), 5, 0, 1 << 20, smem=1)(
        pos, *exchange(chunk, "x" + side)
    )


def basis_kernel(side, pos_ref, top_ref, low_ref, linv_ref, o_ref):
    p = block_place(pos_ref, pos_ref[PLACE[side]])
    at = pl.ds(pl.multiple_of(lax.rem(p, 2) * 256, 256), 256)
    rows = jnp.where(p < 2, top_ref[at, :], low_ref[at, :])
    o_ref[...] = lax.dot_general(rows, linv_ref[...], (((1,), (1,)), ((), ())), precision=HIGH,
                                 preferred_element_type=F32)


def basis_of(side, pos, top, low, linv):
    return call(functools.partial(basis_kernel, side), f32s(256, 256), 4, 12 << 24, 1 << 20,
                smem=1)(pos, top, low, linv)


def cores_kernel(pos_ref, p_ref, *refs):
    blocks, o_ref = refs[:4], refs[4]
    mask = block_mask(192)
    for i, first in enumerate(ORDER):
        for j, second in enumerate(ORDER):
            source = chunk_at(pos_ref, first, second)
            wide = jnp.where(mask, jnp.concatenate([p_ref[source]] * 12, axis=0), 0.0)
            q = blocks[i][j * 192 : j * 192 + 192, :]
            core = jnp.dot(wide, q, precision=HIGH, preferred_element_type=F32)
            o_ref[pl.ds(source * 12, 12)] = core.reshape(12, 16, 256)


def join_kernel(b0, b1, b2, b3, o_ref):
    for i, b in enumerate((b0, b1, b2, b3)):
        o_ref[i * 192 : (i + 1) * 192, :] = b[...]


def gather_all(value):
    joined = call(join_kernel, f32s(768, 256), 4, 0, 2 << 20)(*exchange(value, "zy"))
    return exchange(joined, "yz")


def refit(side, pos, factors, turned, coupling):
    cross = CROSS[side] * 2
    half = add_up(side, pos, *update(factors, exchange(coupling, cross)))
    rest = send(half, "core")
    piece = sum(exchange(gram(pos, half, rest), cross))
    pieces = deliver(project(turned, half, rest), cross)
    return half, rest, inverse_factor(pos, piece, send(piece, "core")), pieces


def column_scale(ranks):
    positions = jnp.arange(PADDED_RANK, dtype=jnp.int32)
    live = positions[None, :] < ranks[:, None]
    factor = 4.0 / jnp.sqrt(ranks.astype(F32))
    return jnp.where(live, factor[:, None], F32(0.0)).reshape(-1, 1)


def shards(up, down, ranks, left, right):
    adapter, row = lax.axis_index("adapter"), lax.axis_index("row")
    c = adapter % 2
    pos = jnp.stack([adapter // 2, c, row // 4, row % 4]).astype(jnp.int32)
    scale = column_scale(lax.dynamic_slice_in_dim(ranks, row * 12, 12, 0))

    left_rows, right_rows = spread(LEFT, pos, left), spread(RIGHT, pos, right)
    up_turned, down_turned = lay_out(LEFT, pos, up), lay_out(RIGHT, pos, down)
    left_pieces = deliver(project(up_turned, left_rows), CROSS[LEFT] * 2)
    right_pieces = deliver(project(down_turned, right_rows), CROSS[RIGHT] * 2)
    up, down = (
        [
            turned[:, j * 192 : j * 192 + 192].transpose(0, 2, 1).reshape(1024, 192)
            for j in range(4)
        ]
        for turned in (up_turned, down_turned)
    )
    side = f32s(192, 256)
    coupling, p, q = call(first_kernel, [side] * 3, 9, 1 << 28, 3 << 20)(
        *left_pieces, *right_pieces, scale
    )

    step = call(next_kernel, [side] * 2, 7, 1 << 29, 3 << 20)
    for sweep in range(ITERS):
        top, low, linv, pieces = refit(LEFT, pos, up, up_turned, coupling)
        if sweep == ITERS - 1:
            left = basis_of(LEFT, pos, top, low, linv)
        coupling, p = step(*pieces, linv, scale, q)
        if sweep == ITERS - 1:
            p_rows = lax.all_to_all(p.T.reshape(16, 16, 192), "row", 0, 0)
        top, low, linv, pieces = refit(RIGHT, pos, down, down_turned, coupling)
        if sweep == ITERS - 1:
            right = basis_of(RIGHT, pos, top, low, linv)
            q = call(last_kernel, side, 6, 1 << 28, 2 << 20)(*pieces, linv, scale)
        else:
            coupling, q = step(*pieces, linv, scale, p)
    cores = call(cores_kernel, f32s(192, 16, 256), 6, 1 << 30, 6 << 20, smem=1)(
        pos, p_rows, *gather_all(q)
    )
    return left, right, cores


def solution(mesh):
    return jax.shard_map(
        shards,
        mesh=mesh,
        in_specs=(
            P("row", "adapter"),
            P("row", "adapter"),
            P("adapter"),
            P("row", None),
            P("row", None),
        ),
        out_specs=(P("row", None), P("row", None), P("adapter", "row", None)),
        check_vma=False,
    )
```

```python
import functools

import jax
import jax.numpy as jnp
from jax import lax
from jax.experimental import pallas as pl
from jax.experimental.pallas import tpu as pltpu
from jax.sharding import PartitionSpec as P

PADDED_RANK = 16
ITERS = 2
RING = 4
K = 256
PANEL = 32
ORDER = (0, 1, 3, 2)
HIGH = lax.Precision.HIGHEST
F32 = jnp.float32
BF16 = jnp.bfloat16
VMEM = pl.BlockSpec(memory_space=pltpu.VMEM)
SMEM = pl.BlockSpec(memory_space=pltpu.SMEM)
PARAMS = pltpu.CompilerParams(vmem_limit_bytes=8 * 1024 * 1024)


def call(kernel, outs, n_in, flops, nbytes, scratch=(), smem=0):
    return pl.pallas_call(
        kernel,
        out_shape=outs,
        in_specs=[SMEM] * smem + [VMEM] * (n_in - smem),
        out_specs=jax.tree.map(lambda _: VMEM, outs),
        scratch_shapes=list(scratch),
        compiler_params=PARAMS,
        cost_estimate=pl.CostEstimate(flops=flops, bytes_accessed=nbytes, transcendentals=0),
    )


def f32s(*shape):
    return jax.ShapeDtypeStruct(shape, F32)


def moved(axis, d, x, c, z, y):
    if axis == "core":
        return x, 1 - c, z, y
    if axis[c] == "x":
        return (x + d) % RING, c, z, y
    if axis[c] == "y":
        return x, c, z, (y + d) % RING
    return x, c, (z + d) % RING, y


def send(value, axis, d=1):
    perm = []
    for i in range(128):
        x, c, z, y = moved(axis, d, i // 32, i // 16 % 2, i // 4 % 4, i % 4)
        perm.append((i, x * 32 + c * 16 + z * 4 + y))
    return lax.ppermute(value, ("adapter", "row"), perm)


def exchange(value, axis):
    return [value] + [send(value, axis, d) for d in ORDER[1:]]


def deliver(values, axis, sign=-1):
    return [values[0]] + [send(v, axis, sign * d) for d, v in zip(ORDER[1:], values[1:])]


def back(place, d):
    return lax.rem(place + RING - d, RING)


def chunk_at(pos_ref, first, second):
    c, z, y = pos_ref[1], pos_ref[2], pos_ref[3]
    dy = jnp.where(c == 0, first, second)
    dz = jnp.where(c == 0, second, first)
    return back(z, dz) * RING + back(y, dy)


LEFT, RIGHT = "y", "z"
PLACE = {"z": 2, "y": 3}
CROSS = {"y": "z", "z": "y"}


def block_place(pos_ref, place):
    return lax.bitwise_xor(place // 2, pos_ref[1]) * 2 + lax.rem(place, 2)


def split3(value):
    high = value.astype(BF16)
    rest = value - high.astype(F32)
    mid = rest.astype(BF16)
    return high, mid, (rest - mid.astype(F32)).astype(BF16)


def pieces_kernel(side, pos_ref, a_ref, basis_ref, *o_refs):
    at, cross = pos_ref[PLACE[side]], pos_ref[PLACE[CROSS[side]]]
    for o_ref, d in zip(o_refs, ORDER):
        mine = lax.rem(at + d, RING)
        for j, e in enumerate(ORDER):
            theirs = back(cross, e)
            source = theirs * RING + mine if side == "y" else mine * RING + theirs
            o_ref[j * 192 : j * 192 + 192, :] = a_ref[source].astype(F32)
        o_ref[768:, :] = basis_ref[...]


def pieces_of(side, pos, factors, basis):
    return call(functools.partial(pieces_kernel, side), [f32s(1024, 256)] * 4, 3, 0, 6 << 20,
                smem=1)(pos, factors.T.reshape(16, 192, 256), basis)


def straight_kernel(piece_ref, o_ref):
    o_ref[...] = piece_ref[:768, :].T.astype(BF16)


def straighten(piece):
    return call(straight_kernel, jax.ShapeDtypeStruct((256, 768), BF16), 1, 0, 2 << 20)(piece)


def digest_kernel(last, piece_ref, *refs):
    before, (turned_ref, *o_refs) = refs[: -5 if last else -2], refs[-5 if last else -2 :]
    turned = piece_ref[:768, :].astype(BF16)
    turned_ref[...] = turned
    parts = split3(piece_ref[768:, :])
    total = sum(jnp.dot(turned, part, preferred_element_type=F32) for part in reversed(parts))
    for r in before:
        total = r[...] + total
    rows = 768 // len(o_refs)
    for j, o_ref in enumerate(o_refs):
        o_ref[...] = total[j * rows : j * rows + rows]


def digest(piece, before, last=False):
    outs = [jax.ShapeDtypeStruct((768, 256), BF16)]
    outs += [f32s(192, 256)] * 4 if last else [f32s(768, 256)]
    turned, *total = call(functools.partial(digest_kernel, last), outs, 1 + len(before),
                          3 * 768 << 17, 3 << 20)(piece, *before)
    return turned, total


def lay_out(left, right):
    left, right = lax.optimization_barrier((left, right))
    right = deliver(right, RIGHT * 2, 1)
    waiting, right[1] = lax.optimization_barrier((left[3], right[1]))
    left = deliver([*left[:3], waiting], LEFT * 2, 1)
    turned = {LEFT: [], RIGHT: []}
    total = {LEFT: (), RIGHT: ()}
    for i in range(3):
        for side, pieces in ((LEFT, left), (RIGHT, right)):
            block, total[side] = digest(pieces[i], total[side])
            turned[side].append(block)
    right[3], total[LEFT] = lax.optimization_barrier((right[3], total[LEFT]))
    for side, pieces in ((RIGHT, right), (LEFT, left)):
        block, total[side] = digest(pieces[3], total[side], last=True)
        turned[side].append(block)
    return [
        (turned[side], [straighten(p) for p in pieces], total[side])
        for side, pieces in ((LEFT, left), (RIGHT, right))
    ]


def row_places(side, pos_ref):
    return [
        pl.ds(pl.multiple_of(block_place(pos_ref, back(pos_ref[PLACE[side]], d)) * 256, 256), 256)
        for d in ORDER
    ]


def project_kernel(side, pos_ref, a0, a1, a2, a3, top_ref, low_ref, *refs):
    *o_refs, m_ref = refs
    m_ref[:512, :] = top_ref[...]
    m_ref[512:, :] = low_ref[...]
    parts = split3(jnp.concatenate([m_ref[at, :] for at in row_places(side, pos_ref)], axis=0))
    for j, o_ref in enumerate(o_refs):
        block = jnp.concatenate([a[j * 192 : j * 192 + 192, :] for a in (a0, a1, a2, a3)], axis=1)
        o_ref[...] = sum(
            jnp.dot(block, part, preferred_element_type=F32) for part in reversed(parts)
        )


def project(side, pos, turned, top, low):
    return call(functools.partial(project_kernel, side), [f32s(192, 256)] * 4, 7,
                6 * 3072 << 16, 4 << 20, [pltpu.VMEM((1024, 256), F32)], smem=1)(
        pos, *turned, top, low
    )


def gram_kernel(pos_ref, rows_ref, *refs):
    mine = rows_ref[:, pl.ds(pl.multiple_of(pos_ref[1] * 128, 128), 128)]
    total = lax.dot_general(mine, rows_ref[...], (((0,), (0,)), ((), ())), precision=HIGH,
                            preferred_element_type=F32)
    refs[-1][...] = refs[0][...] + total if len(refs) == 2 else total


def gram(pos, rows, *before):
    return call(gram_kernel, f32s(128, 256), 2 + len(before), 12 << 24, 1 << 19, smem=1)(
        pos, rows, *before
    )


def eliminate(tall, at):
    n = tall.shape[0]
    sub = lax.broadcasted_iota(jnp.int32, (n, 128), 0)
    lane = lax.broadcasted_iota(jnp.int32, (n, 128), 1)
    half, base = at // 128, at % 128
    columns = [
        jnp.broadcast_to(tall[:, at + k : at + k + 1], (n, 128)) for k in range(8)
    ]
    sides = [tall[:, :128], tall[:, 128:]]
    pivots = jnp.ones((8, 128), F32)
    for j in range(8):
        pivot = columns[j][j : j + 1, :]
        times = jnp.where(sub > j, columns[j], 0.0) * (1.0 / pivot)
        pivots = jnp.where(sub[:8] == j, pivot, pivots)
        for k in range(j + 1, 8):
            columns[k] = columns[k] - times * columns[k][j : j + 1, :]
        here = lane == base + j
        kept = jnp.where(here & (sub >= j), jnp.where(sub == j, 1.0, 0.0), sides[half])
        other = sides[1 - half]
        sides[half] = kept - times * kept[j : j + 1, :]
        sides[1 - half] = other - times * other[j : j + 1, :]
    return jnp.concatenate(sides, axis=1), pivots


def inverse_kernel(pos_ref, mine_ref, mate_ref, o_ref, w_ref):
    for c, ref in ((pos_ref[1], mine_ref), (1 - pos_ref[1], mate_ref)):
        w_ref[pl.ds(pl.multiple_of(c * 128, 128), 128), :] = ref[...]
    lane = lax.broadcasted_iota(jnp.int32, (PANEL, K), 1)
    row = lax.broadcasted_iota(jnp.int32, (PANEL, K), 0)
    all_lane = lax.broadcasted_iota(jnp.int32, (K, K), 1)
    all_row = lax.broadcasted_iota(jnp.int32, (K, K), 0)
    for lo in range(0, K, PANEL):
        hi = lo + PANEL
        rest = w_ref[lo:hi, :]
        done, pivots = [], []
        for at in range(lo, hi, 8):
            rest, found = eliminate(rest, at)
            done.append(rest[:8])
            pivots.append(found)
            rest = rest[8:]
        r = jnp.concatenate(done, axis=0)
        pivots = jnp.concatenate(pivots, axis=0)
        pivots = jnp.concatenate([pivots, pivots], axis=1)
        clean = jnp.where((lane < hi) & (lane > row + lo), 0.0, r)
        o_ref[lo:hi, :] = jnp.where(lane <= row + lo, clean, 0.0) * lax.rsqrt(pivots)
        if hi < K:
            times = jnp.where(lane >= hi, r, 0.0) / pivots
            change = jnp.dot(times.T, clean, precision=HIGH, preferred_element_type=F32)
            gone = (all_lane >= lo) & (all_lane < hi) & (all_row >= hi)
            w_ref[...] = jnp.where(gone, 0.0, w_ref[...]) - change


def inverse_factor(pos, mine, mate):
    return call(inverse_kernel, f32s(K, K), 3, 0, 1 << 10,
                [pltpu.VMEM((K, K), F32)], smem=1)(pos, mine, mate)


def block_mask(n):
    rows = lax.broadcasted_iota(jnp.int32, (n, n), 0) // PADDED_RANK
    return rows == lax.broadcasted_iota(jnp.int32, (n, n), 1) // PADDED_RANK


def couple(own, other, scale):
    small = lax.dot_general(other, other, (((1,), (1,)), ((), ())), precision=HIGH,
                            preferred_element_type=F32)
    small = jnp.where(block_mask(192), small, 0.0)
    return jnp.dot(small, own, precision=HIGH, preferred_element_type=F32) * scale


def first_kernel(*refs):
    left, right = refs[0:4], refs[4:8]
    scale_ref, c_ref, p_ref, q_ref = refs[8:]
    scale = scale_ref[...]
    p, q = (sum(r[...] for r in side) * scale for side in (left, right))
    c_ref[...] = couple(p, q, scale)
    p_ref[...] = p
    q_ref[...] = q


def normalised(pieces, linv_ref, scale):
    return lax.dot_general(sum(r[...] for r in pieces), linv_ref[...], (((1,), (1,)), ((), ())),
                           precision=HIGH, preferred_element_type=F32) * scale


def next_kernel(*refs):
    linv_ref, scale_ref, other_ref, c_ref, p_ref = refs[4:]
    scale = scale_ref[...]
    p = normalised(refs[:4], linv_ref, scale)
    c_ref[...] = couple(other_ref[...], p, scale)
    p_ref[...] = p


def last_kernel(*refs):
    linv_ref, scale_ref, q_ref = refs[4:]
    q_ref[...] = normalised(refs[:4], linv_ref, scale_ref[...])


def product(factors, at, blocks):
    a = jnp.concatenate([f[:, at : at + 384] for f in factors], axis=0)
    b = jnp.concatenate([b[...] for b in blocks], axis=0)
    return sum(jnp.dot(a, part, preferred_element_type=F32) for part in reversed(split3(b)))


def early_kernel(a0, a1, a2, a3, b0, b1, o_ref):
    o_ref[...] = product((a0, a1, a2, a3), 0, (b0, b1))


def late_kernel(side, pos_ref, a0, a1, a2, a3, b2, b3, part_ref, keep_ref, send_ref, m_ref):
    total = part_ref[...] + product((a0, a1, a2, a3), 384, (b2, b3))
    for i, at in enumerate(row_places(side, pos_ref)):
        m_ref[at, :] = total[i * 256 : i * 256 + 256]
    keep_ref[...] = m_ref[:512, :]
    send_ref[...] = m_ref[512:, :]


def update(side, pos, straight, blocks):
    part = call(early_kernel, f32s(1024, 256), 6, 3 * 3072 << 16, 3 << 20)(*straight, *blocks[:2])
    return call(functools.partial(late_kernel, side), [f32s(512, 256)] * 2, 8, 3 * 3072 << 16,
                3 << 20, [pltpu.VMEM((1024, 256), F32)], smem=1)(
        pos, *straight, *blocks[2:], part
    )


def first_place(side, pos_ref):
    return jnp.where(pos_ref[1] == 0, pos_ref[0], pos_ref[PLACE[side]])


def split_kernel(side, pos_ref, keep_ref, other_ref, *o_refs):
    for o_ref, d in zip(o_refs, ORDER):
        at = pl.multiple_of(back(first_place(side, pos_ref), d) * 128, 128)
        o_ref[...] = keep_ref[pl.ds(at, 128), :] + other_ref[pl.ds(at, 128), :]


def merge_kernel(side, pos_ref, *refs):
    for r, d in zip(refs[:-1], ORDER):
        at = pl.multiple_of(back(first_place(side, pos_ref), d) * 128, 128)
        refs[-1][pl.ds(at, 128), :] = r[...]


def add_up(side, pos, keep, other):
    chunks = call(functools.partial(split_kernel, side), [f32s(128, 256)] * 4, 3, 0, 2 << 20,
                  smem=1)(pos, keep, send(other, "core"))
    chunk = sum(deliver(chunks, "x" + side))
    chunk = sum(exchange(chunk, side + "x"))
    return call(functools.partial(merge_kernel, side), f32s(512, 256), 5, 0, 1 << 20, smem=1)(
        pos, *exchange(chunk, "x" + side)
    )


def basis_kernel(side, pos_ref, top_ref, low_ref, linv_ref, o_ref):
    p = block_place(pos_ref, pos_ref[PLACE[side]])
    at = pl.ds(pl.multiple_of(lax.rem(p, 2) * 256, 256), 256)
    rows = jnp.where(p < 2, top_ref[at, :], low_ref[at, :])
    o_ref[...] = lax.dot_general(rows, linv_ref[...], (((1,), (1,)), ((), ())), precision=HIGH,
                                 preferred_element_type=F32)


def basis_of(side, pos, top, low, linv):
    return call(functools.partial(basis_kernel, side), f32s(256, 256), 4, 12 << 24, 1 << 20,
                smem=1)(pos, top, low, linv)


def cores_kernel(pos_ref, p_ref, *refs):
    blocks, o_ref = refs[:4], refs[4]
    mask = block_mask(192)
    for i, first in enumerate(ORDER):
        for j, second in enumerate(ORDER):
            source = chunk_at(pos_ref, first, second)
            wide = jnp.where(mask, jnp.concatenate([p_ref[source]] * 12, axis=0), 0.0)
            p_high, p_mid, unused = split3(wide)
            q_high, q_mid, unused = split3(blocks[i][j * 192 : j * 192 + 192, :])
            core = sum(
                jnp.dot(p, q, preferred_element_type=F32)
                for p, q in ((p_mid, q_high), (p_high, q_mid), (p_high, q_high))
            )
            o_ref[pl.ds(source * 12, 12)] = core.reshape(12, 16, 256)


def join_kernel(b0, b1, b2, b3, o_ref):
    for i, b in enumerate((b0, b1, b2, b3)):
        o_ref[i * 192 : (i + 1) * 192, :] = b[...]


def gather_all(value):
    joined = call(join_kernel, f32s(768, 256), 4, 0, 2 << 20)(*exchange(value, "zy"))
    return exchange(joined, "yz")


def refit(side, pos, straight, turned, coupling):
    cross = CROSS[side] * 2
    half = add_up(side, pos, *update(side, pos, straight, exchange(coupling, cross)))
    rest = send(half, "core")
    piece = sum(exchange(gram(pos, rest, gram(pos, half)), cross))
    pieces = deliver(project(side, pos, turned, half, rest), cross)
    return half, rest, inverse_factor(pos, piece, send(piece, "core")), pieces


def column_scale(ranks):
    positions = jnp.arange(PADDED_RANK, dtype=jnp.int32)
    live = positions[None, :] < ranks[:, None]
    factor = 4.0 / jnp.sqrt(ranks.astype(F32))
    return jnp.where(live, factor[:, None], F32(0.0)).reshape(-1, 1)


def shards(up, down, ranks, left, right):
    adapter, row = lax.axis_index("adapter"), lax.axis_index("row")
    c = adapter % 2
    pos = jnp.stack([adapter // 2, c, row // 4, row % 4]).astype(jnp.int32)
    scale = column_scale(lax.dynamic_slice_in_dim(ranks, row * 12, 12, 0))

    sides = lay_out(pieces_of(LEFT, pos, up, left), pieces_of(RIGHT, pos, down, right))
    (up_turned, up, left_chunks), (down_turned, down, right_chunks) = sides
    left_pieces = deliver(left_chunks, CROSS[LEFT] * 2)
    right_pieces = deliver(right_chunks, CROSS[RIGHT] * 2)
    side = f32s(192, 256)
    coupling, p, q = call(first_kernel, [side] * 3, 9, 1 << 28, 3 << 20)(
        *left_pieces, *right_pieces, scale
    )

    step = call(next_kernel, [side] * 2, 7, 1 << 29, 3 << 20)
    for sweep in range(ITERS):
        top, low, linv, pieces = refit(LEFT, pos, up, up_turned, coupling)
        if sweep == ITERS - 1:
            left = basis_of(LEFT, pos, top, low, linv)
        coupling, p = step(*pieces, linv, scale, q)
        if sweep == ITERS - 1:
            p_rows = lax.all_to_all(p.T.reshape(16, 16, 192), "row", 0, 0)
        top, low, linv, pieces = refit(RIGHT, pos, down, down_turned, coupling)
        if sweep == ITERS - 1:
            right = basis_of(RIGHT, pos, top, low, linv)
            q = call(last_kernel, side, 6, 1 << 28, 2 << 20)(*pieces, linv, scale)
        else:
            coupling, q = step(*pieces, linv, scale, p)
    cores = call(cores_kernel, f32s(192, 16, 256), 6, 1 << 30, 6 << 20, smem=1)(
        pos, p_rows, *gather_all(q)
    )
    return left, right, cores


def solution(mesh):
    return jax.shard_map(
        shards,
        mesh=mesh,
        in_specs=(
            P("row", "adapter"),
            P("row", "adapter"),
            P("adapter"),
            P("row", None),
            P("row", None),
        ),
        out_specs=(P("row", None), P("row", None), P("adapter", "row", None)),
        check_vma=False,
    )
```

```python
import functools

import jax
import jax.numpy as jnp
from jax import lax
from jax.experimental import pallas as pl
from jax.experimental.pallas import tpu as pltpu
from jax.sharding import PartitionSpec as P

PADDED_RANK = 16
ITERS = 2
RING = 4
K = 256
PANEL = 32
STEP = 16
ORDER = (0, 1, 3, 2)
HIGH = lax.Precision.HIGHEST
F32 = jnp.float32
BF16 = jnp.bfloat16
VMEM = pl.BlockSpec(memory_space=pltpu.VMEM)
SMEM = pl.BlockSpec(memory_space=pltpu.SMEM)
PARAMS = pltpu.CompilerParams(vmem_limit_bytes=8 * 1024 * 1024)


def call(kernel, outs, n_in, flops, nbytes, scratch=(), smem=0):
    return pl.pallas_call(
        kernel,
        out_shape=outs,
        in_specs=[SMEM] * smem + [VMEM] * (n_in - smem),
        out_specs=jax.tree.map(lambda _: VMEM, outs),
        scratch_shapes=list(scratch),
        compiler_params=PARAMS,
        cost_estimate=pl.CostEstimate(flops=flops, bytes_accessed=nbytes, transcendentals=0),
    )


def f32s(*shape):
    return jax.ShapeDtypeStruct(shape, F32)


def moved(axis, d, x, c, z, y):
    if axis == "core":
        return x, 1 - c, z, y
    if axis[c] == "x":
        return (x + d) % RING, c, z, y
    if axis[c] == "y":
        return x, c, z, (y + d) % RING
    return x, c, (z + d) % RING, y


def send(value, axis, d=1):
    perm = []
    for i in range(128):
        x, c, z, y = moved(axis, d, i // 32, i // 16 % 2, i // 4 % 4, i % 4)
        perm.append((i, x * 32 + c * 16 + z * 4 + y))
    return lax.ppermute(value, ("adapter", "row"), perm)


def exchange(value, axis):
    return [value] + [send(value, axis, d) for d in ORDER[1:]]


def deliver(values, axis, sign=-1):
    return [values[0]] + [send(v, axis, sign * d) for d, v in zip(ORDER[1:], values[1:])]


def back(place, d):
    return lax.rem(place + RING - d, RING)


def chunk_at(pos_ref, first, second):
    c, z, y = pos_ref[1], pos_ref[2], pos_ref[3]
    dy = jnp.where(c == 0, first, second)
    dz = jnp.where(c == 0, second, first)
    return back(z, dz) * RING + back(y, dy)


LEFT, RIGHT = "y", "z"
PLACE = {"z": 2, "y": 3}
CROSS = {"y": "z", "z": "y"}


def block_place(pos_ref, place):
    return lax.bitwise_xor(place // 2, pos_ref[1]) * 2 + lax.rem(place, 2)


def split3(value):
    high = value.astype(BF16)
    rest = value - high.astype(F32)
    mid = rest.astype(BF16)
    return high, mid, (rest - mid.astype(F32)).astype(BF16)


def split2(value):
    high = value.astype(BF16)
    return high, (value - high.astype(F32)).astype(BF16)


def pieces_kernel(side, pos_ref, a_ref, basis_ref, *o_refs):
    at, cross = pos_ref[PLACE[side]], pos_ref[PLACE[CROSS[side]]]
    for o_ref, d in zip(o_refs, ORDER):
        mine = lax.rem(at + d, RING)
        for j, e in enumerate(ORDER):
            theirs = back(cross, e)
            source = theirs * RING + mine if side == "y" else mine * RING + theirs
            o_ref[j * 192 : j * 192 + 192, :] = a_ref[source].astype(F32)
        o_ref[768:, :] = basis_ref[...]


def pieces_of(side, pos, factors, basis):
    return call(functools.partial(pieces_kernel, side), [f32s(1024, 256)] * 4, 3, 0, 6 << 20,
                smem=1)(pos, factors.T.reshape(16, 192, 256), basis)


def straight_kernel(piece_ref, o_ref):
    o_ref[...] = piece_ref[:768, :].T.astype(BF16)


def straighten(piece):
    return call(straight_kernel, jax.ShapeDtypeStruct((256, 768), BF16), 1, 0, 2 << 20)(piece)


def digest_kernel(last, piece_ref, *refs):
    before, (turned_ref, *o_refs) = refs[: -5 if last else -2], refs[-5 if last else -2 :]
    turned = piece_ref[:768, :].astype(BF16)
    turned_ref[...] = turned
    parts = split2(piece_ref[768:, :])
    total = sum(jnp.dot(turned, part, preferred_element_type=F32) for part in reversed(parts))
    for r in before:
        total = r[...] + total
    rows = 768 // len(o_refs)
    for j, o_ref in enumerate(o_refs):
        o_ref[...] = total[j * rows : j * rows + rows]


def digest(piece, before, last=False):
    outs = [jax.ShapeDtypeStruct((768, 256), BF16)]
    outs += [f32s(192, 256)] * 4 if last else [f32s(768, 256)]
    turned, *total = call(functools.partial(digest_kernel, last), outs, 1 + len(before),
                          3 * 768 << 17, 3 << 20)(piece, *before)
    return turned, total


def lay_out(left, right):
    left, right = lax.optimization_barrier((left, right))
    right = deliver(right, RIGHT * 2, 1)
    waiting, right[1] = lax.optimization_barrier((left[3], right[1]))
    left = deliver([*left[:3], waiting], LEFT * 2, 1)
    turned = {LEFT: [], RIGHT: []}
    total = {LEFT: (), RIGHT: ()}
    for i in range(3):
        for side, pieces in ((LEFT, left), (RIGHT, right)):
            block, total[side] = digest(pieces[i], total[side])
            turned[side].append(block)
    right[3], total[LEFT] = lax.optimization_barrier((right[3], total[LEFT]))
    for side, pieces in ((RIGHT, right), (LEFT, left)):
        block, total[side] = digest(pieces[3], total[side], last=True)
        turned[side].append(block)
    return [
        (turned[side], [straighten(p) for p in pieces], total[side])
        for side, pieces in ((LEFT, left), (RIGHT, right))
    ]


def row_places(side, pos_ref):
    return [
        pl.ds(pl.multiple_of(block_place(pos_ref, back(pos_ref[PLACE[side]], d)) * 256, 256), 256)
        for d in ORDER
    ]


def place_chunks(side, pos_ref, chunks, m_ref):
    for i, r in enumerate(chunks):
        c = pos_ref[1] if i < 4 else 1 - pos_ref[1]
        at = i // 4 * 512 + back(first_place(side, pos_ref, c), ORDER[i % 4]) * 128
        m_ref[pl.ds(pl.multiple_of(at, 128), 128), :] = r[...]


def project_kernel(side, pos_ref, a0, a1, a2, a3, *refs):
    chunks, o_refs, m_ref = refs[:8], refs[8:12], refs[12]
    place_chunks(side, pos_ref, chunks, m_ref)
    parts = split2(jnp.concatenate([m_ref[at, :] for at in row_places(side, pos_ref)], axis=0))
    for j, o_ref in enumerate(o_refs):
        block = jnp.concatenate([a[j * 192 : j * 192 + 192, :] for a in (a0, a1, a2, a3)], axis=1)
        o_ref[...] = sum(
            jnp.dot(block, part, preferred_element_type=F32) for part in reversed(parts)
        )


def project(side, pos, turned, chunks):
    return call(functools.partial(project_kernel, side), [f32s(192, 256)] * 4, 13,
                4 * 3072 << 16, 4 << 20, [pltpu.VMEM((1024, 256), F32)], smem=1)(
        pos, *turned, *chunks
    )


def gram_kernel(pos_ref, *refs):
    chunks, before, o_ref = refs[:4], refs[4:-1], refs[-1]
    rows = jnp.concatenate([r[...] for r in chunks], axis=0)
    at = pl.ds(pl.multiple_of(pos_ref[1] * 128, 128), 128)
    mine = jnp.concatenate([r[:, at] for r in chunks], axis=0)
    total = lax.dot_general(mine, rows, (((0,), (0,)), ((), ())), precision=HIGH,
                            preferred_element_type=F32)
    for r in before:
        total = r[...] + total
    o_ref[...] = total


def gram(pos, chunks, *before):
    return call(gram_kernel, f32s(128, 256), 5 + len(before), 12 << 24, 1 << 19, smem=1)(
        pos, *chunks, *before
    )


def eliminate(tall, at):
    n = tall.shape[0]
    sub = lax.broadcasted_iota(jnp.int32, (n, 128), 0)
    lane = lax.broadcasted_iota(jnp.int32, (n, 128), 1)
    half, base = at // 128, at % 128
    columns = [
        jnp.broadcast_to(tall[:, at + k : at + k + 1], (n, 128)) for k in range(STEP)
    ]
    sides = [tall[:, :128], tall[:, 128:]]
    pivots = jnp.ones((STEP, 128), F32)
    for j in range(STEP):
        pivot = columns[j][j : j + 1, :]
        times = jnp.where(sub > j, columns[j], 0.0) * (1.0 / pivot)
        pivots = jnp.where(sub[:STEP] == j, pivot, pivots)
        for k in range(j + 1, STEP):
            columns[k] = columns[k] - times * columns[k][j : j + 1, :]
        here = lane == base + j
        kept = jnp.where(here & (sub >= j), jnp.where(sub == j, 1.0, 0.0), sides[half])
        other = sides[1 - half]
        sides[half] = kept - times * kept[j : j + 1, :]
        sides[1 - half] = other - times * other[j : j + 1, :]
    return jnp.concatenate(sides, axis=1), pivots


def narrow_product(left, right):
    left, right = split3(left), split3(right)
    order = ((2, 0), (0, 2), (1, 1), (1, 0), (0, 1), (0, 0))
    return lax.dot_general(
        jnp.concatenate([left[i] for i, j in order], axis=0),
        jnp.concatenate([right[j] for i, j in order], axis=0),
        (((0,), (0,)), ((), ())),
        preferred_element_type=F32,
    )


def inverse_kernel(pos_ref, mine_ref, mate_ref, o_ref, w_ref):
    for c, ref in ((pos_ref[1], mine_ref), (1 - pos_ref[1], mate_ref)):
        w_ref[pl.ds(pl.multiple_of(c * 128, 128), 128), :] = ref[...]
    lane = lax.broadcasted_iota(jnp.int32, (PANEL, K), 1)
    row = lax.broadcasted_iota(jnp.int32, (PANEL, K), 0)
    for lo in range(0, K, PANEL):
        hi = lo + PANEL
        rest = w_ref[lo:hi, :]
        done, pivots = [], []
        for at in range(lo, hi, STEP):
            rest, found = eliminate(rest, at)
            done.append(rest[:STEP])
            pivots.append(found)
            rest = rest[STEP:]
        r = jnp.concatenate(done, axis=0)
        pivots = jnp.concatenate(pivots, axis=0)
        pivots = jnp.concatenate([pivots, pivots], axis=1)
        clean = jnp.where((lane < hi) & (lane > row + lo), 0.0, r)
        o_ref[lo:hi, :] = jnp.where(lane <= row + lo, clean, 0.0) * lax.rsqrt(pivots)
        if hi < K:
            start = hi // 128 * 128
            change = narrow_product((r / pivots)[:, start:], clean)
            rows = w_ref[hi:, :]
            lanes = lax.broadcasted_iota(jnp.int32, rows.shape, 1)
            kept = jnp.where((lanes >= lo) & (lanes < hi), 0.0, rows)
            w_ref[hi:, :] = kept - change[hi - start :]


def inverse_factor(pos, mine, mate):
    return call(inverse_kernel, f32s(K, K), 3, 0, 1 << 10,
                [pltpu.VMEM((K, K), F32)], smem=1)(pos, mine, mate)


def block_mask(n):
    rows = lax.broadcasted_iota(jnp.int32, (n, n), 0) // PADDED_RANK
    return rows == lax.broadcasted_iota(jnp.int32, (n, n), 1) // PADDED_RANK


def couple(own, other, scale):
    small = lax.dot_general(other, other, (((1,), (1,)), ((), ())), precision=HIGH,
                            preferred_element_type=F32)
    small = jnp.where(block_mask(192), small, 0.0)
    return jnp.dot(small, own, precision=HIGH, preferred_element_type=F32) * scale


def first_kernel(*refs):
    left, right = refs[0:4], refs[4:8]
    scale_ref, c_ref, p_ref, q_ref = refs[8:]
    scale = scale_ref[...]
    p, q = (sum(r[...] for r in side) * scale for side in (left, right))
    c_ref[...] = couple(p, q, scale)
    p_ref[...] = p
    q_ref[...] = q


def normalised(pieces, linv_ref, scale):
    return lax.dot_general(sum(r[...] for r in pieces), linv_ref[...], (((1,), (1,)), ((), ())),
                           precision=HIGH, preferred_element_type=F32) * scale


def next_kernel(*refs):
    linv_ref, scale_ref, other_ref, c_ref, p_ref = refs[4:]
    scale = scale_ref[...]
    p = normalised(refs[:4], linv_ref, scale)
    c_ref[...] = couple(other_ref[...], p, scale)
    p_ref[...] = p


def last_kernel(*refs):
    linv_ref, scale_ref, q_ref = refs[4:]
    q_ref[...] = normalised(refs[:4], linv_ref, scale_ref[...])


def product(factors, at, blocks):
    a = jnp.concatenate([f[:, at : at + 384] for f in factors], axis=0)
    b = jnp.concatenate([b[...] for b in blocks], axis=0)
    return sum(jnp.dot(a, part, preferred_element_type=F32) for part in reversed(split2(b)))


def early_kernel(a0, a1, a2, a3, b0, b1, o_ref):
    o_ref[...] = product((a0, a1, a2, a3), 0, (b0, b1))


def late_kernel(side, pos_ref, a0, a1, a2, a3, b2, b3, part_ref, *refs):
    o_refs, m_ref = refs[:8], refs[8]
    total = part_ref[...] + product((a0, a1, a2, a3), 384, (b2, b3))
    for i, at in enumerate(row_places(side, pos_ref)):
        m_ref[at, :] = total[i * 256 : i * 256 + 256]
    for i, o_ref in enumerate(o_refs):
        c = pos_ref[1] if i < 4 else 1 - pos_ref[1]
        at = i // 4 * 512 + back(first_place(side, pos_ref, c), ORDER[i % 4]) * 128
        o_ref[...] = m_ref[pl.ds(pl.multiple_of(at, 128), 128), :]


def update(side, pos, straight, blocks):
    part = call(early_kernel, f32s(1024, 256), 6, 2 * 3072 << 16, 3 << 20)(*straight, *blocks[:2])
    return call(functools.partial(late_kernel, side), [f32s(128, 256)] * 8, 8, 2 * 3072 << 16,
                3 << 20, [pltpu.VMEM((1024, 256), F32)], smem=1)(
        pos, *straight, *blocks[2:], part
    )


def first_place(side, pos_ref, c):
    return jnp.where(c == 0, pos_ref[0], pos_ref[PLACE[side]])


def add_up(side, chunks):
    chunks = [mine + send(other, "core") for mine, other in zip(chunks[:4], chunks[4:])]
    chunk = sum(deliver(chunks, "x" + side))
    chunk = sum(exchange(chunk, side + "x"))
    return exchange(chunk, "x" + side)


def basis_kernel(side, pos_ref, *refs):
    chunks, linv_ref, o_ref, m_ref = refs[:8], refs[8], refs[9], refs[10]
    place_chunks(side, pos_ref, chunks, m_ref)
    at = block_place(pos_ref, pos_ref[PLACE[side]]) * 256
    rows = m_ref[pl.ds(pl.multiple_of(at, 256), 256), :]
    o_ref[...] = lax.dot_general(rows, linv_ref[...], (((1,), (1,)), ((), ())), precision=HIGH,
                                 preferred_element_type=F32)


def basis_of(side, pos, chunks, linv):
    return call(functools.partial(basis_kernel, side), f32s(256, 256), 10, 12 << 24, 1 << 20,
                [pltpu.VMEM((1024, 256), F32)], smem=1)(pos, *chunks, linv)


def cores_kernel(pos_ref, p_ref, *refs):
    blocks, o_ref = refs[:4], refs[4]
    mask = block_mask(192)
    for i, first in enumerate(ORDER):
        for j, second in enumerate(ORDER):
            source = chunk_at(pos_ref, first, second)
            wide = jnp.where(mask, jnp.concatenate([p_ref[source]] * 12, axis=0), 0.0)
            p_high, p_mid, unused = split3(wide)
            q_high, q_mid, unused = split3(blocks[i][j * 192 : j * 192 + 192, :])
            core = sum(
                jnp.dot(p, q, preferred_element_type=F32)
                for p, q in ((p_mid, q_high), (p_high, q_mid), (p_high, q_high))
            )
            o_ref[pl.ds(source * 12, 12)] = core.reshape(12, 16, 256)


def join_kernel(b0, b1, b2, b3, o_ref):
    for i, b in enumerate((b0, b1, b2, b3)):
        o_ref[i * 192 : (i + 1) * 192, :] = b[...]


def gather_all(value):
    joined = call(join_kernel, f32s(768, 256), 4, 0, 2 << 20)(*exchange(value, "zy"))
    return exchange(joined, "yz")


def refit(side, pos, straight, turned, coupling):
    cross = CROSS[side] * 2
    half = add_up(side, update(side, pos, straight, exchange(coupling, cross)))
    rest = [send(chunk, "core") for chunk in half]
    piece = sum(exchange(gram(pos, rest, gram(pos, half)), cross))
    pieces = deliver(project(side, pos, turned, half + rest), cross)
    return half + rest, inverse_factor(pos, piece, send(piece, "core")), pieces


def column_scale(ranks):
    positions = jnp.arange(PADDED_RANK, dtype=jnp.int32)
    live = positions[None, :] < ranks[:, None]
    factor = 4.0 / jnp.sqrt(ranks.astype(F32))
    return jnp.where(live, factor[:, None], F32(0.0)).reshape(-1, 1)


def shards(up, down, ranks, left, right):
    adapter, row = lax.axis_index("adapter"), lax.axis_index("row")
    c = adapter % 2
    pos = jnp.stack([adapter // 2, c, row // 4, row % 4]).astype(jnp.int32)
    scale = column_scale(lax.dynamic_slice_in_dim(ranks, row * 12, 12, 0))

    sides = lay_out(pieces_of(LEFT, pos, up, left), pieces_of(RIGHT, pos, down, right))
    (up_turned, up, left_chunks), (down_turned, down, right_chunks) = sides
    left_pieces = deliver(left_chunks, CROSS[LEFT] * 2)
    right_pieces = deliver(right_chunks, CROSS[RIGHT] * 2)
    side = f32s(192, 256)
    coupling, p, q = call(first_kernel, [side] * 3, 9, 1 << 28, 3 << 20)(
        *left_pieces, *right_pieces, scale
    )

    step = call(next_kernel, [side] * 2, 7, 1 << 29, 3 << 20)
    for sweep in range(ITERS):
        chunks, linv, pieces = refit(LEFT, pos, up, up_turned, coupling)
        if sweep == ITERS - 1:
            left = basis_of(LEFT, pos, chunks, linv)
        coupling, p = step(*pieces, linv, scale, q)
        if sweep == ITERS - 1:
            p_rows = lax.all_to_all(p.T.reshape(16, 16, 192), "row", 0, 0)
        chunks, linv, pieces = refit(RIGHT, pos, down, down_turned, coupling)
        if sweep == ITERS - 1:
            right = basis_of(RIGHT, pos, chunks, linv)
            q = call(last_kernel, side, 6, 1 << 28, 2 << 20)(*pieces, linv, scale)
        else:
            coupling, q = step(*pieces, linv, scale, p)
    cores = call(cores_kernel, f32s(192, 16, 256), 6, 1 << 30, 6 << 20, smem=1)(
        pos, p_rows, *gather_all(q)
    )
    return left, right, cores


def solution(mesh):
    return jax.shard_map(
        shards,
        mesh=mesh,
        in_specs=(
            P("row", "adapter"),
            P("row", "adapter"),
            P("adapter"),
            P("row", None),
            P("row", None),
        ),
        out_specs=(P("row", None), P("row", None), P("adapter", "row", None)),
        check_vma=False,
    )
```

```python
import functools

import jax
import jax.numpy as jnp
from jax import lax
from jax.experimental import pallas as pl
from jax.experimental.pallas import tpu as pltpu
from jax.sharding import PartitionSpec as P

PADDED_RANK = 16
ITERS = 2
RING = 4
K = 256
PANEL = 32
STEP = 16
ORDER = (0, 1, 3, 2)
HIGH = lax.Precision.HIGHEST
F32 = jnp.float32
BF16 = jnp.bfloat16
VMEM = pl.BlockSpec(memory_space=pltpu.VMEM)
SMEM = pl.BlockSpec(memory_space=pltpu.SMEM)
PARAMS = pltpu.CompilerParams(vmem_limit_bytes=8 * 1024 * 1024)


def call(kernel, outs, n_in, flops, nbytes, scratch=(), smem=0):
    return pl.pallas_call(
        kernel,
        out_shape=outs,
        in_specs=[SMEM] * smem + [VMEM] * (n_in - smem),
        out_specs=jax.tree.map(lambda _: VMEM, outs),
        scratch_shapes=list(scratch),
        compiler_params=PARAMS,
        cost_estimate=pl.CostEstimate(flops=flops, bytes_accessed=nbytes, transcendentals=0),
    )


def f32s(*shape):
    return jax.ShapeDtypeStruct(shape, F32)


def moved(axis, d, x, c, z, y):
    if axis == "core":
        return x, 1 - c, z, y
    if axis[c] == "x":
        return (x + d) % RING, c, z, y
    if axis[c] == "y":
        return x, c, z, (y + d) % RING
    return x, c, (z + d) % RING, y


def send(value, axis, d=1):
    perm = []
    for i in range(128):
        x, c, z, y = moved(axis, d, i // 32, i // 16 % 2, i // 4 % 4, i % 4)
        perm.append((i, x * 32 + c * 16 + z * 4 + y))
    return lax.ppermute(value, ("adapter", "row"), perm)


def exchange(value, axis):
    return [value] + [send(value, axis, d) for d in ORDER[1:]]


def deliver(values, axis, sign=-1):
    return [values[0]] + [send(v, axis, sign * d) for d, v in zip(ORDER[1:], values[1:])]


def back(place, d):
    return lax.rem(place + RING - d, RING)


def chunk_at(pos_ref, first, second):
    c, z, y = pos_ref[1], pos_ref[2], pos_ref[3]
    dy = jnp.where(c == 0, first, second)
    dz = jnp.where(c == 0, second, first)
    return back(z, dz) * RING + back(y, dy)


LEFT, RIGHT = "y", "z"
PLACE = {"z": 2, "y": 3}
CROSS = {"y": "z", "z": "y"}


def block_place(pos_ref, place):
    return lax.bitwise_xor(place // 2, pos_ref[1]) * 2 + lax.rem(place, 2)


def split3(value):
    high = value.astype(BF16)
    rest = value - high.astype(F32)
    mid = rest.astype(BF16)
    return high, mid, (rest - mid.astype(F32)).astype(BF16)


def split2(value):
    high = value.astype(BF16)
    return high, (value - high.astype(F32)).astype(BF16)


def pieces_kernel(side, pos_ref, a_ref, basis_ref, *o_refs):
    at, cross = pos_ref[PLACE[side]], pos_ref[PLACE[CROSS[side]]]
    for o_ref, d in zip(o_refs, ORDER):
        mine = lax.rem(at + d, RING)
        for j, e in enumerate(ORDER):
            theirs = back(cross, e)
            source = theirs * RING + mine if side == "y" else mine * RING + theirs
            o_ref[j * 192 : j * 192 + 192, :] = a_ref[source].astype(F32)
        o_ref[768:, :] = basis_ref[...]


def pieces_of(side, pos, factors, basis):
    return call(functools.partial(pieces_kernel, side), [f32s(1024, 256)] * 4, 3, 0, 6 << 20,
                smem=1)(pos, factors.T.reshape(16, 192, 256), basis)


def straight_kernel(piece_ref, o_ref):
    o_ref[...] = piece_ref[:768, :].T.astype(BF16)


def straighten(piece):
    return call(straight_kernel, jax.ShapeDtypeStruct((256, 768), BF16), 1, 0, 2 << 20)(piece)


def digest_kernel(last, piece_ref, *refs):
    before, (turned_ref, *o_refs) = refs[: -5 if last else -2], refs[-5 if last else -2 :]
    turned = piece_ref[:768, :].astype(BF16)
    turned_ref[...] = turned
    parts = split2(piece_ref[768:, :])
    total = sum(jnp.dot(turned, part, preferred_element_type=F32) for part in reversed(parts))
    for r in before:
        total = r[...] + total
    rows = 768 // len(o_refs)
    for j, o_ref in enumerate(o_refs):
        o_ref[...] = total[j * rows : j * rows + rows]


def digest(piece, before, last=False):
    outs = [jax.ShapeDtypeStruct((768, 256), BF16)]
    outs += [f32s(192, 256)] * 4 if last else [f32s(768, 256)]
    turned, *total = call(functools.partial(digest_kernel, last), outs, 1 + len(before),
                          3 * 768 << 17, 3 << 20)(piece, *before)
    return turned, total


def lay_out(left, right):
    left, right = lax.optimization_barrier((left, right))
    right = deliver(right, RIGHT * 2, 1)
    *left, waiting = left
    left = deliver(left, LEFT * 2, 1)
    waiting, left[1] = lax.optimization_barrier((waiting, left[1]))
    left.append(send(waiting, LEFT * 2, ORDER[3]))
    turned = {LEFT: [], RIGHT: []}
    total = {LEFT: (), RIGHT: ()}
    for i in range(3):
        for side, pieces in ((LEFT, left), (RIGHT, right)):
            block, total[side] = digest(pieces[i], total[side])
            turned[side].append(block)
    right[3], total[LEFT] = lax.optimization_barrier((right[3], total[LEFT]))
    for side, pieces in ((RIGHT, right), (LEFT, left)):
        block, total[side] = digest(pieces[3], total[side], last=True)
        turned[side].append(block)
    return [
        (turned[side], [straighten(p) for p in pieces], total[side])
        for side, pieces in ((LEFT, left), (RIGHT, right))
    ]


def row_places(side, pos_ref):
    return [
        pl.ds(pl.multiple_of(block_place(pos_ref, back(pos_ref[PLACE[side]], d)) * 256, 256), 256)
        for d in ORDER
    ]


def place_chunks(side, pos_ref, chunks, m_ref):
    for i, r in enumerate(chunks):
        c = pos_ref[1] if i < 4 else 1 - pos_ref[1]
        at = i // 4 * 512 + back(first_place(side, pos_ref, c), ORDER[i % 4]) * 128
        m_ref[pl.ds(pl.multiple_of(at, 128), 128), :] = r[...]


def project_kernel(side, pos_ref, a0, a1, a2, a3, *refs):
    chunks, o_refs, rows_ref, m_ref = refs[:8], refs[8:12], refs[12], refs[13]
    place_chunks(side, pos_ref, chunks, m_ref)
    places = row_places(side, pos_ref)
    rows_ref[...] = m_ref[places[0], :]
    parts = split2(jnp.concatenate([m_ref[at, :] for at in places], axis=0))
    for j, o_ref in enumerate(o_refs):
        block = jnp.concatenate([a[j * 192 : j * 192 + 192, :] for a in (a0, a1, a2, a3)], axis=1)
        o_ref[...] = sum(
            jnp.dot(block, part, preferred_element_type=F32) for part in reversed(parts)
        )


def project(side, pos, turned, chunks):
    return call(functools.partial(project_kernel, side), [f32s(192, 256)] * 4 + [f32s(256, 256)],
                13, 4 * 3072 << 16, 4 << 20, [pltpu.VMEM((1024, 256), F32)], smem=1)(
        pos, *turned, *chunks
    )


def gram_kernel(pos_ref, *refs):
    chunks, before, o_ref = refs[:4], refs[4:-1], refs[-1]
    rows = jnp.concatenate([r[...] for r in chunks], axis=0)
    at = pl.ds(pl.multiple_of(pos_ref[1] * 128, 128), 128)
    mine = jnp.concatenate([r[:, at] for r in chunks], axis=0)
    total = lax.dot_general(mine, rows, (((0,), (0,)), ((), ())), precision=HIGH,
                            preferred_element_type=F32)
    for r in before:
        total = r[...] + total
    o_ref[...] = total


def gram(pos, chunks, *before):
    return call(gram_kernel, f32s(128, 256), 5 + len(before), 12 << 24, 1 << 19, smem=1)(
        pos, *chunks, *before
    )


def eliminate(tall, at):
    n = tall.shape[0]
    sub = lax.broadcasted_iota(jnp.int32, (n, 128), 0)
    lane = lax.broadcasted_iota(jnp.int32, (n, 128), 1)
    half, base = at // 128, at % 128
    columns = [
        jnp.broadcast_to(tall[:, at + k : at + k + 1], (n, 128)) for k in range(STEP)
    ]
    sides = [tall[:, :128], tall[:, 128:]]
    pivots = jnp.ones((STEP, 128), F32)
    for j in range(STEP):
        pivot = columns[j][j : j + 1, :]
        times = jnp.where(sub > j, columns[j], 0.0) * (1.0 / pivot)
        pivots = jnp.where(sub[:STEP] == j, pivot, pivots)
        for k in range(j + 1, STEP):
            columns[k] = columns[k] - times * columns[k][j : j + 1, :]
        here = lane == base + j
        kept = jnp.where(here & (sub >= j), jnp.where(sub == j, 1.0, 0.0), sides[half])
        other = sides[1 - half]
        sides[half] = kept - times * kept[j : j + 1, :]
        sides[1 - half] = other - times * other[j : j + 1, :]
    return jnp.concatenate(sides, axis=1), pivots


def narrow_product(left, right):
    left, right = split3(left), split3(right)
    order = ((2, 0), (0, 2), (1, 1), (1, 0), (0, 1), (0, 0))
    return lax.dot_general(
        jnp.concatenate([left[i] for i, j in order], axis=0),
        jnp.concatenate([right[j] for i, j in order], axis=0),
        (((0,), (0,)), ((), ())),
        preferred_element_type=F32,
    )


def inverse_kernel(pos_ref, mine_ref, mate_ref, o_ref, w_ref):
    for c, ref in ((pos_ref[1], mine_ref), (1 - pos_ref[1], mate_ref)):
        w_ref[pl.ds(pl.multiple_of(c * 128, 128), 128), :] = ref[...]
    lane = lax.broadcasted_iota(jnp.int32, (PANEL, K), 1)
    row = lax.broadcasted_iota(jnp.int32, (PANEL, K), 0)
    for lo in range(0, K, PANEL):
        hi = lo + PANEL
        rest = w_ref[lo:hi, :]
        done, pivots = [], []
        for at in range(lo, hi, STEP):
            rest, found = eliminate(rest, at)
            done.append(rest[:STEP])
            pivots.append(found)
            rest = rest[STEP:]
        r = jnp.concatenate(done, axis=0)
        pivots = jnp.concatenate(pivots, axis=0)
        pivots = jnp.concatenate([pivots, pivots], axis=1)
        clean = jnp.where((lane < hi) & (lane > row + lo), 0.0, r)
        o_ref[lo:hi, :] = jnp.where(lane <= row + lo, clean, 0.0) * lax.rsqrt(pivots)
        if hi < K:
            start = hi // 128 * 128
            change = narrow_product((r / pivots)[:, start:], clean)
            rows = w_ref[hi:, :]
            lanes = lax.broadcasted_iota(jnp.int32, rows.shape, 1)
            kept = jnp.where((lanes >= lo) & (lanes < hi), 0.0, rows)
            w_ref[hi:, :] = kept - change[hi - start :]


def inverse_factor(pos, mine, mate):
    return call(inverse_kernel, f32s(K, K), 3, 0, 1 << 10,
                [pltpu.VMEM((K, K), F32)], smem=1)(pos, mine, mate)


def block_mask(n):
    rows = lax.broadcasted_iota(jnp.int32, (n, n), 0) // PADDED_RANK
    return rows == lax.broadcasted_iota(jnp.int32, (n, n), 1) // PADDED_RANK


def couple(own, other, scale):
    small = lax.dot_general(other, other, (((1,), (1,)), ((), ())), precision=HIGH,
                            preferred_element_type=F32)
    small = jnp.where(block_mask(192), small, 0.0)
    return jnp.dot(small, own, precision=HIGH, preferred_element_type=F32) * scale


def first_kernel(*refs):
    left, right = refs[0:4], refs[4:8]
    scale_ref, c_ref, p_ref, q_ref = refs[8:]
    scale = scale_ref[...]
    p, q = (sum(r[...] for r in side) * scale for side in (left, right))
    c_ref[...] = couple(p, q, scale)
    p_ref[...] = p
    q_ref[...] = q


def normalised(pieces, linv_ref, scale):
    return lax.dot_general(sum(r[...] for r in pieces), linv_ref[...], (((1,), (1,)), ((), ())),
                           precision=HIGH, preferred_element_type=F32) * scale


def next_kernel(*refs):
    linv_ref, scale_ref, other_ref, c_ref, p_ref = refs[4:]
    scale = scale_ref[...]
    p = normalised(refs[:4], linv_ref, scale)
    c_ref[...] = couple(other_ref[...], p, scale)
    p_ref[...] = p


def last_kernel(*refs):
    linv_ref, scale_ref, q_ref = refs[4:]
    q_ref[...] = normalised(refs[:4], linv_ref, scale_ref[...])


def product(factors, at, blocks):
    a = jnp.concatenate([f[:, at : at + 384] for f in factors], axis=0)
    b = jnp.concatenate([b[...] for b in blocks], axis=0)
    return sum(jnp.dot(a, part, preferred_element_type=F32) for part in reversed(split2(b)))


def early_kernel(a0, a1, a2, a3, b0, b1, o_ref):
    o_ref[...] = product((a0, a1, a2, a3), 0, (b0, b1))


def late_kernel(side, pos_ref, a0, a1, a2, a3, b2, b3, part_ref, *refs):
    o_refs, m_ref = refs[:8], refs[8]
    total = part_ref[...] + product((a0, a1, a2, a3), 384, (b2, b3))
    for i, at in enumerate(row_places(side, pos_ref)):
        m_ref[at, :] = total[i * 256 : i * 256 + 256]
    for i, o_ref in enumerate(o_refs):
        c = pos_ref[1] if i < 4 else 1 - pos_ref[1]
        at = i // 4 * 512 + back(first_place(side, pos_ref, c), ORDER[i % 4]) * 128
        o_ref[...] = m_ref[pl.ds(pl.multiple_of(at, 128), 128), :]


def update(side, pos, straight, blocks):
    part = call(early_kernel, f32s(1024, 256), 6, 2 * 3072 << 16, 3 << 20)(*straight, *blocks[:2])
    return call(functools.partial(late_kernel, side), [f32s(128, 256)] * 8, 8, 2 * 3072 << 16,
                3 << 20, [pltpu.VMEM((1024, 256), F32)], smem=1)(
        pos, *straight, *blocks[2:], part
    )


def first_place(side, pos_ref, c):
    return jnp.where(c == 0, pos_ref[0], pos_ref[PLACE[side]])


def add_up(side, chunks):
    chunks = [mine + send(other, "core") for mine, other in zip(chunks[:4], chunks[4:])]
    chunk = sum(deliver(chunks, "x" + side))
    chunk = sum(exchange(chunk, side + "x"))
    return exchange(chunk, "x" + side)


def basis_kernel(rows_ref, linv_ref, o_ref):
    o_ref[...] = lax.dot_general(rows_ref[...], linv_ref[...], (((1,), (1,)), ((), ())),
                                 precision=HIGH, preferred_element_type=F32)


def basis_of(rows, linv):
    return call(basis_kernel, f32s(256, 256), 2, 12 << 24, 1 << 20)(rows, linv)


def cores_kernel(pos_ref, p_ref, *refs):
    blocks, o_ref, core_ref, sems = refs[:4], refs[4], refs[5], refs[6]
    mask = block_mask(192)
    copies = []
    for i, first in enumerate(ORDER):
        for j, second in enumerate(ORDER):
            source = chunk_at(pos_ref, first, second)
            wide = jnp.where(mask, jnp.concatenate([p_ref[source]] * 12, axis=0), 0.0)
            p_high, p_low = split2(wide)
            q_high, q_low = split2(blocks[i][j * 192 : j * 192 + 192, :])
            core = sum(
                jnp.dot(p, q, preferred_element_type=F32)
                for p, q in ((p_low, q_high), (p_high, q_low), (p_high, q_high))
            )
            at = i * RING + j
            core_ref[at] = core.reshape(12, 16, 256)
            copies.append(
                pltpu.make_async_copy(
                    core_ref.at[at], o_ref.at[pl.ds(source * 12, 12)], sems.at[at]
                )
            )
            copies[-1].start()
    for copy in copies:
        copy.wait()


def cores_of(pos, p_rows, blocks):
    return pl.pallas_call(
        cores_kernel,
        out_shape=f32s(192, 16, 256),
        in_specs=[SMEM] + [VMEM] * 5,
        out_specs=pl.BlockSpec(memory_space=pl.ANY),
        scratch_shapes=[
            pltpu.VMEM((16, 12, 16, 256), F32), pltpu.SemaphoreType.DMA((16,))
        ],
        compiler_params=PARAMS,
        cost_estimate=pl.CostEstimate(flops=1 << 30, bytes_accessed=6 << 20, transcendentals=0),
    )(pos, p_rows, *blocks)


def join_kernel(b0, b1, b2, b3, o_ref):
    for i, b in enumerate((b0, b1, b2, b3)):
        o_ref[i * 192 : (i + 1) * 192, :] = b[...]


def gather_all(value):
    joined = call(join_kernel, f32s(768, 256), 4, 0, 2 << 20)(*exchange(value, "zy"))
    return exchange(joined, "yz")


def refit(side, pos, straight, turned, coupling, beside=()):
    cross = CROSS[side] * 2
    *blocks, last = exchange(coupling, cross)
    last, *beside = lax.optimization_barrier((last, *beside))
    half = add_up(side, update(side, pos, straight, [*blocks, last]))
    rest = [send(chunk, "core") for chunk in half]
    piece = sum(exchange(gram(pos, rest, gram(pos, half)), cross))
    *pieces, rows = project(side, pos, turned, half + rest)
    linv = inverse_factor(pos, piece, send(piece, "core"))
    return rows, linv, deliver(pieces, cross), beside


def column_scale(ranks):
    positions = jnp.arange(PADDED_RANK, dtype=jnp.int32)
    live = positions[None, :] < ranks[:, None]
    factor = 4.0 / jnp.sqrt(ranks.astype(F32))
    return jnp.where(live, factor[:, None], F32(0.0)).reshape(-1, 1)


def shards(up, down, ranks, left, right):
    adapter, row = lax.axis_index("adapter"), lax.axis_index("row")
    c = adapter % 2
    pos = jnp.stack([adapter // 2, c, row // 4, row % 4]).astype(jnp.int32)
    scale = column_scale(lax.dynamic_slice_in_dim(ranks, row * 12, 12, 0))

    sides = lay_out(pieces_of(LEFT, pos, up, left), pieces_of(RIGHT, pos, down, right))
    (up_turned, up, left_chunks), (down_turned, down, right_chunks) = sides
    left_pieces = deliver(left_chunks, CROSS[LEFT] * 2)
    right_pieces = deliver(right_chunks, CROSS[RIGHT] * 2)
    side = f32s(192, 256)
    coupling, p, q = call(first_kernel, [side] * 3, 9, 1 << 28, 3 << 20)(
        *left_pieces, *right_pieces, scale
    )

    step = call(next_kernel, [side] * 2, 7, 1 << 29, 3 << 20)
    beside = ()
    for sweep in range(ITERS):
        rows, linv, pieces, unused = refit(LEFT, pos, up, up_turned, coupling)
        coupling, p = step(*pieces, linv, scale, q)
        if sweep == ITERS - 1:
            beside = (basis_of(rows, linv),)
            p_rows = lax.all_to_all(p.T.reshape(16, 16, 192), "row", 0, 0)
        rows, linv, pieces, beside = refit(RIGHT, pos, down, down_turned, coupling, beside)
        if sweep < ITERS - 1:
            coupling, q = step(*pieces, linv, scale, p)
    q = call(last_kernel, side, 6, 1 << 28, 2 << 20)(*pieces, linv, scale)
    return beside[0], basis_of(rows, linv), cores_of(pos, p_rows, gather_all(q))


def solution(mesh):
    return jax.shard_map(
        shards,
        mesh=mesh,
        in_specs=(
            P("row", "adapter"),
            P("row", "adapter"),
            P("adapter"),
            P("row", None),
            P("row", None),
        ),
        out_specs=(P("row", None), P("row", None), P("adapter", "row", None)),
        check_vma=False,
    )
```

```python
import functools

import jax
import jax.numpy as jnp
from jax import lax
from jax.experimental import pallas as pl
from jax.experimental.pallas import tpu as pltpu
from jax.sharding import PartitionSpec as P

PADDED_RANK = 16
ITERS = 2
RING = 4
K = 256
PANEL = 32
STEP = 16
ORDER = (0, 1, 3, 2)
HIGH = lax.Precision.HIGHEST
SIX = ((2, 0), (0, 2), (1, 1), (1, 0), (0, 1), (0, 0))
THREE = ((1, 0), (0, 1), (0, 0))
F32 = jnp.float32
BF16 = jnp.bfloat16
VMEM = pl.BlockSpec(memory_space=pltpu.VMEM)
SMEM = pl.BlockSpec(memory_space=pltpu.SMEM)
PARAMS = pltpu.CompilerParams(vmem_limit_bytes=8 * 1024 * 1024)


def call(kernel, outs, n_in, flops, nbytes, scratch=(), smem=0):
    return pl.pallas_call(
        kernel,
        out_shape=outs,
        in_specs=[SMEM] * smem + [VMEM] * (n_in - smem),
        out_specs=jax.tree.map(lambda _: VMEM, outs),
        scratch_shapes=list(scratch),
        compiler_params=PARAMS,
        cost_estimate=pl.CostEstimate(flops=flops, bytes_accessed=nbytes, transcendentals=0),
    )


def f32s(*shape):
    return jax.ShapeDtypeStruct(shape, F32)


def moved(axis, d, x, c, z, y):
    if axis == "core":
        return x, 1 - c, z, y
    if axis[c] == "x":
        return (x + d) % RING, c, z, y
    if axis[c] == "y":
        return x, c, z, (y + d) % RING
    return x, c, (z + d) % RING, y


def send(value, axis, d=1):
    perm = []
    for i in range(128):
        x, c, z, y = moved(axis, d, i // 32, i // 16 % 2, i // 4 % 4, i % 4)
        perm.append((i, x * 32 + c * 16 + z * 4 + y))
    return lax.ppermute(value, ("adapter", "row"), perm)


def exchange(value, axis):
    return [value] + [send(value, axis, d) for d in ORDER[1:]]


def deliver(values, axis, sign=-1):
    return [values[0]] + [send(v, axis, sign * d) for d, v in zip(ORDER[1:], values[1:])]


def back(place, d):
    return lax.rem(place + RING - d, RING)


def chunk_at(pos_ref, first, second):
    c, z, y = pos_ref[1], pos_ref[2], pos_ref[3]
    dy = jnp.where(c == 0, first, second)
    dz = jnp.where(c == 0, second, first)
    return back(z, dz) * RING + back(y, dy)


LEFT, RIGHT = "y", "z"
PLACE = {"z": 2, "y": 3}
CROSS = {"y": "z", "z": "y"}


def block_place(pos_ref, place):
    return lax.bitwise_xor(place // 2, pos_ref[1]) * 2 + lax.rem(place, 2)


def split3(value):
    high = value.astype(BF16)
    rest = value - high.astype(F32)
    mid = rest.astype(BF16)
    return high, mid, (rest - mid.astype(F32)).astype(BF16)


def split2(value):
    high = value.astype(BF16)
    return high, (value - high.astype(F32)).astype(BF16)


def pieces_kernel(side, pos_ref, a_ref, basis_ref, *o_refs):
    at, cross = pos_ref[PLACE[side]], pos_ref[PLACE[CROSS[side]]]
    for o_ref, d in zip(o_refs, ORDER):
        mine = lax.rem(at + d, RING)
        for j, e in enumerate(ORDER):
            theirs = back(cross, e)
            source = theirs * RING + mine if side == "y" else mine * RING + theirs
            o_ref[j * 192 : j * 192 + 192, :] = a_ref[source].astype(F32)
        o_ref[768:, :] = basis_ref[...]


def pieces_of(side, pos, factors, basis):
    return call(functools.partial(pieces_kernel, side), [f32s(1024, 256)] * 4, 3, 0, 6 << 20,
                smem=1)(pos, factors.T.reshape(16, 192, 256), basis)


def straight_kernel(piece_ref, o_ref):
    o_ref[...] = piece_ref[:768, :].T.astype(BF16)


def straighten(piece):
    return call(straight_kernel, jax.ShapeDtypeStruct((256, 768), BF16), 1, 0, 2 << 20)(piece)


def digest_kernel(last, piece_ref, *refs):
    before, (turned_ref, *o_refs) = refs[: -5 if last else -2], refs[-5 if last else -2 :]
    turned = piece_ref[:768, :].astype(BF16)
    turned_ref[...] = turned
    parts = split2(piece_ref[768:, :])
    total = sum(jnp.dot(turned, part, preferred_element_type=F32) for part in reversed(parts))
    for r in before:
        total = r[...] + total
    rows = 768 // len(o_refs)
    for j, o_ref in enumerate(o_refs):
        o_ref[...] = total[j * rows : j * rows + rows]


def digest(piece, before, last=False):
    outs = [jax.ShapeDtypeStruct((768, 256), BF16)]
    outs += [f32s(192, 256)] * 4 if last else [f32s(768, 256)]
    turned, *total = call(functools.partial(digest_kernel, last), outs, 1 + len(before),
                          3 * 768 << 17, 3 << 20)(piece, *before)
    return turned, total


def lay_out(left, right):
    left, right = lax.optimization_barrier((left, right))
    right = deliver(right, RIGHT * 2, 1)
    *left, waiting = left
    left = deliver(left, LEFT * 2, 1)
    waiting, left[1] = lax.optimization_barrier((waiting, left[1]))
    left.append(send(waiting, LEFT * 2, ORDER[3]))
    turned = {LEFT: [], RIGHT: []}
    total = {LEFT: (), RIGHT: ()}
    for i in range(3):
        for side, pieces in ((LEFT, left), (RIGHT, right)):
            block, total[side] = digest(pieces[i], total[side])
            turned[side].append(block)
    right[3], total[LEFT] = lax.optimization_barrier((right[3], total[LEFT]))
    for side, pieces in ((RIGHT, right), (LEFT, left)):
        block, total[side] = digest(pieces[3], total[side], last=True)
        turned[side].append(block)
    return [
        (turned[side], [straighten(p) for p in pieces], total[side])
        for side, pieces in ((LEFT, left), (RIGHT, right))
    ]


def row_places(side, pos_ref):
    return [
        pl.ds(pl.multiple_of(block_place(pos_ref, back(pos_ref[PLACE[side]], d)) * 256, 256), 256)
        for d in ORDER
    ]


def place_chunks(side, pos_ref, chunks, m_ref):
    for i, r in enumerate(chunks):
        c = pos_ref[1] if i < 4 else 1 - pos_ref[1]
        at = i // 4 * 512 + back(first_place(side, pos_ref, c), ORDER[i % 4]) * 128
        m_ref[pl.ds(pl.multiple_of(at, 128), 128), :] = r[...]


def project_kernel(side, pos_ref, a0, a1, a2, a3, *refs):
    chunks, o_refs, row_refs, m_ref = refs[:8], refs[8:12], refs[12:-1], refs[-1]
    place_chunks(side, pos_ref, chunks, m_ref)
    places = row_places(side, pos_ref)
    for r in row_refs:
        r[...] = m_ref[places[0], :]
    parts = split2(jnp.concatenate([m_ref[at, :] for at in places], axis=0))
    for j, o_ref in enumerate(o_refs):
        block = jnp.concatenate([a[j * 192 : j * 192 + 192, :] for a in (a0, a1, a2, a3)], axis=1)
        o_ref[...] = sum(
            jnp.dot(block, part, preferred_element_type=F32) for part in reversed(parts)
        )


def project(side, pos, turned, chunks, last):
    outs = [f32s(192, 256)] * 4 + [f32s(256, 256)] * last
    return call(functools.partial(project_kernel, side), outs, 13, 4 * 3072 << 16, 4 << 20,
                [pltpu.VMEM((1024, 256), F32)], smem=1)(pos, *turned, *chunks)


def gram_kernel(pos_ref, *refs):
    chunks, before, o_ref = refs[:4], refs[4:-1], refs[-1]
    rows = jnp.concatenate([r[...] for r in chunks], axis=0)
    at = pl.ds(pl.multiple_of(pos_ref[1] * 128, 128), 128)
    mine = jnp.concatenate([r[:, at] for r in chunks], axis=0)
    total = lax.dot_general(mine, rows, (((0,), (0,)), ((), ())), precision=HIGH,
                            preferred_element_type=F32)
    for r in before:
        total = r[...] + total
    o_ref[...] = total


def gram(pos, chunks, *before):
    return call(gram_kernel, f32s(128, 256), 5 + len(before), 12 << 24, 1 << 19, smem=1)(
        pos, *chunks, *before
    )


def eliminate(tall, at):
    n = tall.shape[0]
    sub = lax.broadcasted_iota(jnp.int32, (n, 128), 0)
    lane = lax.broadcasted_iota(jnp.int32, (n, 128), 1)
    half, base = at // 128, at % 128
    columns = [
        jnp.broadcast_to(tall[:, at + k : at + k + 1], (n, 128)) for k in range(STEP)
    ]
    sides = [tall[:, :128], tall[:, 128:]]
    pivots = jnp.ones((STEP, 128), F32)
    for j in range(STEP):
        pivot = columns[j][j : j + 1, :]
        times = jnp.where(sub > j, columns[j], 0.0) * (1.0 / pivot)
        pivots = jnp.where(sub[:STEP] == j, pivot, pivots)
        for k in range(j + 1, STEP):
            columns[k] = columns[k] - times * columns[k][j : j + 1, :]
        here = lane == base + j
        kept = jnp.where(here & (sub >= j), jnp.where(sub == j, 1.0, 0.0), sides[half])
        other = sides[1 - half]
        sides[half] = kept - times * kept[j : j + 1, :]
        sides[1 - half] = other - times * other[j : j + 1, :]
    return jnp.concatenate(sides, axis=1), pivots


def narrow_product(left, right):
    left, right = split3(left), split3(right)
    return lax.dot_general(
        jnp.concatenate([left[i] for i, j in SIX], axis=0),
        jnp.concatenate([right[j] for i, j in SIX], axis=0),
        (((0,), (0,)), ((), ())),
        preferred_element_type=F32,
    )


def inverse_kernel(pos_ref, mine_ref, mate_ref, o_ref, w_ref):
    for c, ref in ((pos_ref[1], mine_ref), (1 - pos_ref[1], mate_ref)):
        w_ref[pl.ds(pl.multiple_of(c * 128, 128), 128), :] = ref[...]
    lane = lax.broadcasted_iota(jnp.int32, (PANEL, K), 1)
    row = lax.broadcasted_iota(jnp.int32, (PANEL, K), 0)
    for lo in range(0, K, PANEL):
        hi = lo + PANEL
        rest = w_ref[lo:hi, :]
        done, pivots = [], []
        for at in range(lo, hi, STEP):
            rest, found = eliminate(rest, at)
            done.append(rest[:STEP])
            pivots.append(found)
            rest = rest[STEP:]
        r = jnp.concatenate(done, axis=0)
        pivots = jnp.concatenate(pivots, axis=0)
        pivots = jnp.concatenate([pivots, pivots], axis=1)
        clean = jnp.where((lane < hi) & (lane > row + lo), 0.0, r)
        o_ref[lo:hi, :] = jnp.where(lane <= row + lo, clean, 0.0) * lax.rsqrt(pivots)
        if hi < K:
            start = hi // 128 * 128
            change = narrow_product((r / pivots)[:, start:], clean)
            rows = w_ref[hi:, :]
            lanes = lax.broadcasted_iota(jnp.int32, rows.shape, 1)
            kept = jnp.where((lanes >= lo) & (lanes < hi), 0.0, rows)
            w_ref[hi:, :] = kept - change[hi - start :]


def inverse_factor(pos, mine, mate):
    return call(inverse_kernel, f32s(K, K), 3, 0, 1 << 10,
                [pltpu.VMEM((K, K), F32)], smem=1)(pos, mine, mate)


def block_mask(n):
    rows = lax.broadcasted_iota(jnp.int32, (n, n), 0) // PADDED_RANK
    return rows == lax.broadcasted_iota(jnp.int32, (n, n), 1) // PADDED_RANK


def three_products(left, right, dims):
    left, right = split2(left), split2(right)
    return sum(
        lax.dot_general(left[i], right[j], (dims, ((), ())), preferred_element_type=F32)
        for i, j in THREE
    )


def couple(own, other, scale):
    small = jnp.where(block_mask(192), three_products(other, other, ((1,), (1,))), 0.0)
    return three_products(small, own, ((1,), (0,))) * scale


def first_kernel(*refs):
    left, right = refs[0:4], refs[4:8]
    scale_ref, c_ref, p_ref, q_ref = refs[8:]
    scale = scale_ref[...]
    p, q = (sum(r[...] for r in side) * scale for side in (left, right))
    c_ref[...] = couple(p, q, scale)
    p_ref[...] = p
    q_ref[...] = q


def normalised(pieces, linv_ref, scale):
    return lax.dot_general(sum(r[...] for r in pieces), linv_ref[...], (((1,), (1,)), ((), ())),
                           precision=HIGH, preferred_element_type=F32) * scale


def next_kernel(*refs):
    linv_ref, scale_ref, other_ref, c_ref, p_ref = refs[4:]
    scale = scale_ref[...]
    p = normalised(refs[:4], linv_ref, scale)
    c_ref[...] = couple(other_ref[...], p, scale)
    p_ref[...] = p


def last_kernel(*refs):
    linv_ref, scale_ref, q_ref = refs[4:]
    q_ref[...] = normalised(refs[:4], linv_ref, scale_ref[...])


def product(factors, at, blocks):
    a = jnp.concatenate([f[:, at : at + 384] for f in factors], axis=0)
    b = jnp.concatenate([b[...] for b in blocks], axis=0)
    return sum(jnp.dot(a, part, preferred_element_type=F32) for part in reversed(split2(b)))


def early_kernel(a0, a1, a2, a3, b0, b1, o_ref):
    o_ref[...] = product((a0, a1, a2, a3), 0, (b0, b1))


def late_kernel(side, pos_ref, a0, a1, a2, a3, b2, b3, part_ref, *refs):
    o_refs, m_ref = refs[:8], refs[8]
    total = part_ref[...] + product((a0, a1, a2, a3), 384, (b2, b3))
    for i, at in enumerate(row_places(side, pos_ref)):
        m_ref[at, :] = total[i * 256 : i * 256 + 256]
    for i, o_ref in enumerate(o_refs):
        c = pos_ref[1] if i < 4 else 1 - pos_ref[1]
        at = i // 4 * 512 + back(first_place(side, pos_ref, c), ORDER[i % 4]) * 128
        o_ref[...] = m_ref[pl.ds(pl.multiple_of(at, 128), 128), :]


def update(side, pos, straight, blocks):
    part = call(early_kernel, f32s(1024, 256), 6, 2 * 3072 << 16, 3 << 20)(*straight, *blocks[:2])
    return call(functools.partial(late_kernel, side), [f32s(128, 256)] * 8, 8, 2 * 3072 << 16,
                3 << 20, [pltpu.VMEM((1024, 256), F32)], smem=1)(
        pos, *straight, *blocks[2:], part
    )


def first_place(side, pos_ref, c):
    return jnp.where(c == 0, pos_ref[0], pos_ref[PLACE[side]])


def add_up(side, chunks):
    chunks = [mine + send(other, "core") for mine, other in zip(chunks[:4], chunks[4:])]
    chunk = sum(deliver(chunks, "x" + side))
    chunk = sum(exchange(chunk, side + "x"))
    return exchange(chunk, "x" + side)


def basis_kernel(rows_ref, linv_ref, o_ref):
    o_ref[...] = lax.dot_general(rows_ref[...], linv_ref[...], (((1,), (1,)), ((), ())),
                                 precision=HIGH, preferred_element_type=F32)


def basis_of(rows, linv):
    return call(basis_kernel, f32s(256, 256), 2, 12 << 24, 1 << 20)(rows, linv)


def cores_kernel(pos_ref, p_ref, *refs):
    blocks, o_ref, core_ref, sems = refs[:4], refs[4], refs[5], refs[6]
    mask = block_mask(192)
    copies = []
    for i, first in enumerate(ORDER):
        for j, second in enumerate(ORDER):
            source = chunk_at(pos_ref, first, second)
            wide = jnp.where(mask, jnp.concatenate([p_ref[source]] * 12, axis=0), 0.0)
            p_high, p_low = split2(wide)
            q_high, q_low = split2(blocks[i][j * 192 : j * 192 + 192, :])
            core = sum(
                jnp.dot(p, q, preferred_element_type=F32)
                for p, q in ((p_low, q_high), (p_high, q_low), (p_high, q_high))
            )
            at = i * RING + j
            core_ref[at] = core.reshape(12, 16, 256)
            copies.append(
                pltpu.make_async_copy(
                    core_ref.at[at], o_ref.at[pl.ds(source * 12, 12)], sems.at[at]
                )
            )
            copies[-1].start()
    for copy in copies:
        copy.wait()


def cores_of(pos, p_rows, blocks):
    return pl.pallas_call(
        cores_kernel,
        out_shape=f32s(192, 16, 256),
        in_specs=[SMEM] + [VMEM] * 5,
        out_specs=pl.BlockSpec(memory_space=pl.ANY),
        scratch_shapes=[
            pltpu.VMEM((16, 12, 16, 256), F32), pltpu.SemaphoreType.DMA((16,))
        ],
        compiler_params=PARAMS,
        cost_estimate=pl.CostEstimate(flops=1 << 30, bytes_accessed=6 << 20, transcendentals=0),
    )(pos, p_rows, *blocks)


def join_kernel(b0, b1, b2, b3, o_ref):
    for i, b in enumerate((b0, b1, b2, b3)):
        o_ref[i * 192 : (i + 1) * 192, :] = b[...]


def gather_all(value):
    joined = call(join_kernel, f32s(768, 256), 4, 0, 2 << 20)(*exchange(value, "zy"))
    return exchange(joined, "yz")


def refit(side, pos, straight, turned, coupling, last_sweep, beside=()):
    cross = CROSS[side] * 2
    *blocks, last = exchange(coupling, cross)
    last, *beside = lax.optimization_barrier((last, *beside))
    half = add_up(side, update(side, pos, straight, [*blocks, last]))
    rest = [send(chunk, "core") for chunk in half]
    piece = sum(exchange(gram(pos, rest, gram(pos, half)), cross))
    projected = project(side, pos, turned, half + rest, last_sweep)
    linv = inverse_factor(pos, piece, send(piece, "core"))
    return projected[4:], linv, deliver(projected[:4], cross), beside


def column_scale(ranks):
    positions = jnp.arange(PADDED_RANK, dtype=jnp.int32)
    live = positions[None, :] < ranks[:, None]
    factor = 4.0 / jnp.sqrt(ranks.astype(F32))
    return jnp.where(live, factor[:, None], F32(0.0)).reshape(-1, 1)


def shards(up, down, ranks, left, right):
    adapter, row = lax.axis_index("adapter"), lax.axis_index("row")
    c = adapter % 2
    pos = jnp.stack([adapter // 2, c, row // 4, row % 4]).astype(jnp.int32)
    scale = column_scale(lax.dynamic_slice_in_dim(ranks, row * 12, 12, 0))

    sides = lay_out(pieces_of(LEFT, pos, up, left), pieces_of(RIGHT, pos, down, right))
    (up_turned, up, left_chunks), (down_turned, down, right_chunks) = sides
    left_pieces = deliver(left_chunks, CROSS[LEFT] * 2)
    right_pieces = deliver(right_chunks, CROSS[RIGHT] * 2)
    side = f32s(192, 256)
    coupling, p, q = call(first_kernel, [side] * 3, 9, 1 << 28, 3 << 20)(
        *left_pieces, *right_pieces, scale
    )

    step = call(next_kernel, [side] * 2, 7, 1 << 29, 3 << 20)
    beside = ()
    for sweep in range(ITERS):
        last = sweep == ITERS - 1
        rows, linv, pieces, unused = refit(LEFT, pos, up, up_turned, coupling, last)
        coupling, p = step(*pieces, linv, scale, q)
        if last:
            beside = (basis_of(*rows, linv),)
            p_rows = lax.all_to_all(p.T.reshape(16, 16, 192), "row", 0, 0)
        rows, linv, pieces, beside = refit(
            RIGHT, pos, down, down_turned, coupling, last, beside
        )
        if not last:
            coupling, q = step(*pieces, linv, scale, p)
    q = call(last_kernel, side, 6, 1 << 28, 2 << 20)(*pieces, linv, scale)
    return beside[0], basis_of(*rows, linv), cores_of(pos, p_rows, gather_all(q))


def solution(mesh):
    return jax.shard_map(
        shards,
        mesh=mesh,
        in_specs=(
            P("row", "adapter"),
            P("row", "adapter"),
            P("adapter"),
            P("row", None),
            P("row", None),
        ),
        out_specs=(P("row", None), P("row", None), P("adapter", "row", None)),
        check_vma=False,
    )
```

```python
import functools

import jax
import jax.numpy as jnp
from jax import lax
from jax.experimental import pallas as pl
from jax.experimental.pallas import tpu as pltpu
from jax.sharding import PartitionSpec as P

PADDED_RANK = 16
ITERS = 2
RING = 4
K = 256
PANEL = 32
STEP = 16
ORDER = (0, 1, 3, 2)
HIGH = lax.Precision.HIGHEST
SIX = ((2, 0), (0, 2), (1, 1), (1, 0), (0, 1), (0, 0))
THREE = ((1, 0), (0, 1), (0, 0))
F32 = jnp.float32
BF16 = jnp.bfloat16
VMEM = pl.BlockSpec(memory_space=pltpu.VMEM)
SMEM = pl.BlockSpec(memory_space=pltpu.SMEM)
PARAMS = pltpu.CompilerParams(vmem_limit_bytes=8 * 1024 * 1024)


def call(kernel, outs, n_in, flops, nbytes, scratch=(), smem=0):
    return pl.pallas_call(
        kernel,
        out_shape=outs,
        in_specs=[SMEM] * smem + [VMEM] * (n_in - smem),
        out_specs=jax.tree.map(lambda _: VMEM, outs),
        scratch_shapes=list(scratch),
        compiler_params=PARAMS,
        cost_estimate=pl.CostEstimate(flops=flops, bytes_accessed=nbytes, transcendentals=0),
    )


def f32s(*shape):
    return jax.ShapeDtypeStruct(shape, F32)


def moved(axis, d, x, c, z, y):
    if axis == "core":
        return x, 1 - c, z, y
    if axis[c] == "x":
        return x ^ d, c, z, y
    if axis[c] == "y":
        return x, c, z, y ^ d
    return x, c, z ^ d, y


def send(value, axis, d=1):
    perm = []
    for i in range(128):
        x, c, z, y = moved(axis, d, i // 32, i // 16 % 2, i // 4 % 4, i % 4)
        perm.append((i, x * 32 + c * 16 + z * 4 + y))
    return lax.ppermute(value, ("adapter", "row"), perm)


def exchange(value, axis):
    return [value] + [send(value, axis, d) for d in ORDER[1:]]


def deliver(values, axis):
    return [values[0]] + [send(v, axis, d) for d, v in zip(ORDER[1:], values[1:])]


def back(place, d):
    return place ^ d


def chunk_at(pos_ref, first, second):
    c, z, y = pos_ref[1], pos_ref[2], pos_ref[3]
    dy = jnp.where(c == 0, first, second)
    dz = jnp.where(c == 0, second, first)
    return back(z, dz) * RING + back(y, dy)


LEFT, RIGHT = "y", "z"
PLACE = {"z": 2, "y": 3}
CROSS = {"y": "z", "z": "y"}


def block_place(pos_ref, place):
    return lax.bitwise_xor(place // 2, pos_ref[1]) * 2 + lax.rem(place, 2)


def split3(value):
    high = value.astype(BF16)
    rest = value - high.astype(F32)
    mid = rest.astype(BF16)
    return high, mid, (rest - mid.astype(F32)).astype(BF16)


def split2(value):
    high = value.astype(BF16)
    return high, (value - high.astype(F32)).astype(BF16)


def pieces_kernel(side, pos_ref, a_ref, basis_ref, *o_refs):
    at, cross = pos_ref[PLACE[side]], pos_ref[PLACE[CROSS[side]]]
    for o_ref, d in zip(o_refs, ORDER):
        mine = back(at, d)
        for j, e in enumerate(ORDER):
            theirs = back(cross, e)
            source = theirs * RING + mine if side == "y" else mine * RING + theirs
            o_ref[j * 192 : j * 192 + 192, :] = a_ref[source].astype(F32)
        o_ref[768:, :] = basis_ref[...]


def pieces_of(side, pos, factors, basis):
    return call(functools.partial(pieces_kernel, side), [f32s(1024, 256)] * 4, 3, 0, 6 << 20,
                smem=1)(pos, factors.T.reshape(16, 192, 256), basis)


def straight_kernel(piece_ref, o_ref):
    o_ref[...] = piece_ref[:768, :].T.astype(BF16)


def straighten(piece):
    return call(straight_kernel, jax.ShapeDtypeStruct((256, 768), BF16), 1, 0, 2 << 20)(piece)


def digest_kernel(last, piece_ref, *refs):
    before, (turned_ref, *o_refs) = refs[: -5 if last else -2], refs[-5 if last else -2 :]
    turned = piece_ref[:768, :].astype(BF16)
    turned_ref[...] = turned
    parts = split2(piece_ref[768:, :])
    total = sum(jnp.dot(turned, part, preferred_element_type=F32) for part in reversed(parts))
    for r in before:
        total = r[...] + total
    rows = 768 // len(o_refs)
    for j, o_ref in enumerate(o_refs):
        o_ref[...] = total[j * rows : j * rows + rows]


def digest(piece, before, last=False):
    outs = [jax.ShapeDtypeStruct((768, 256), BF16)]
    outs += [f32s(192, 256)] * 4 if last else [f32s(768, 256)]
    turned, *total = call(functools.partial(digest_kernel, last), outs, 1 + len(before),
                          3 * 768 << 17, 3 << 20)(piece, *before)
    return turned, total


def lay_out(left, right):
    left, right = lax.optimization_barrier((left, right))
    right = deliver(right, RIGHT * 2)
    *left, waiting = left
    left = deliver(left, LEFT * 2)
    waiting, left[1] = lax.optimization_barrier((waiting, left[1]))
    left.append(send(waiting, LEFT * 2, ORDER[3]))
    turned = {LEFT: [], RIGHT: []}
    total = {LEFT: (), RIGHT: ()}
    for i in range(3):
        for side, pieces in ((LEFT, left), (RIGHT, right)):
            block, total[side] = digest(pieces[i], total[side])
            turned[side].append(block)
    right[3], total[LEFT] = lax.optimization_barrier((right[3], total[LEFT]))
    for side, pieces in ((RIGHT, right), (LEFT, left)):
        block, total[side] = digest(pieces[3], total[side], last=True)
        turned[side].append(block)
    return [
        (turned[side], [straighten(p) for p in pieces], total[side])
        for side, pieces in ((LEFT, left), (RIGHT, right))
    ]


def row_places(side, pos_ref):
    return [
        pl.ds(pl.multiple_of(block_place(pos_ref, back(pos_ref[PLACE[side]], d)) * 256, 256), 256)
        for d in ORDER
    ]


def place_chunks(side, pos_ref, chunks, m_ref):
    for i, r in enumerate(chunks):
        c = pos_ref[1] if i < 4 else 1 - pos_ref[1]
        at = i // 4 * 512 + back(first_place(side, pos_ref, c), ORDER[i % 4]) * 128
        m_ref[pl.ds(pl.multiple_of(at, 128), 128), :] = r[...]


def project_kernel(side, pos_ref, a0, a1, a2, a3, *refs):
    chunks, o_refs, row_refs, m_ref = refs[:8], refs[8:12], refs[12:-1], refs[-1]
    place_chunks(side, pos_ref, chunks, m_ref)
    places = row_places(side, pos_ref)
    for r in row_refs:
        r[...] = m_ref[places[0], :]
    parts = split2(jnp.concatenate([m_ref[at, :] for at in places], axis=0))
    for j, o_ref in enumerate(o_refs):
        block = jnp.concatenate([a[j * 192 : j * 192 + 192, :] for a in (a0, a1, a2, a3)], axis=1)
        o_ref[...] = sum(
            jnp.dot(block, part, preferred_element_type=F32) for part in reversed(parts)
        )


def project(side, pos, turned, chunks, last):
    outs = [f32s(192, 256)] * 4 + [f32s(256, 256)] * last
    return call(functools.partial(project_kernel, side), outs, 13, 4 * 3072 << 16, 4 << 20,
                [pltpu.VMEM((1024, 256), F32)], smem=1)(pos, *turned, *chunks)


def gram_kernel(pos_ref, *refs):
    chunks, before, o_ref = refs[:4], refs[4:-1], refs[-1]
    rows = jnp.concatenate([r[...] for r in chunks], axis=0)
    at = pl.ds(pl.multiple_of(pos_ref[1] * 128, 128), 128)
    mine = jnp.concatenate([r[:, at] for r in chunks], axis=0)
    total = lax.dot_general(mine, rows, (((0,), (0,)), ((), ())), precision=HIGH,
                            preferred_element_type=F32)
    for r in before:
        total = r[...] + total
    o_ref[...] = total


def gram(pos, chunks, *before):
    return call(gram_kernel, f32s(128, 256), 5 + len(before), 12 << 24, 1 << 19, smem=1)(
        pos, *chunks, *before
    )


def eliminate(tall, at):
    n = tall.shape[0]
    sub = lax.broadcasted_iota(jnp.int32, (n, 128), 0)
    lane = lax.broadcasted_iota(jnp.int32, (n, 128), 1)
    half, base = at // 128, at % 128
    columns = [
        jnp.broadcast_to(tall[:, at + k : at + k + 1], (n, 128)) for k in range(STEP)
    ]
    sides = [tall[:, :128], tall[:, 128:]]
    pivots = jnp.ones((STEP, 128), F32)
    for j in range(STEP):
        pivot = columns[j][j : j + 1, :]
        times = jnp.where(sub > j, columns[j], 0.0) * (1.0 / pivot)
        pivots = jnp.where(sub[:STEP] == j, pivot, pivots)
        for k in range(j + 1, STEP):
            columns[k] = columns[k] - times * columns[k][j : j + 1, :]
        here = lane == base + j
        kept = jnp.where(here & (sub >= j), jnp.where(sub == j, 1.0, 0.0), sides[half])
        other = sides[1 - half]
        sides[half] = kept - times * kept[j : j + 1, :]
        sides[1 - half] = other - times * other[j : j + 1, :]
    return jnp.concatenate(sides, axis=1), pivots


def narrow_product(left, right):
    left, right = split3(left), split3(right)
    return lax.dot_general(
        jnp.concatenate([left[i] for i, j in SIX], axis=0),
        jnp.concatenate([right[j] for i, j in SIX], axis=0),
        (((0,), (0,)), ((), ())),
        preferred_element_type=F32,
    )


def inverse_kernel(pos_ref, mine_ref, mate_ref, o_ref, w_ref):
    for c, ref in ((pos_ref[1], mine_ref), (1 - pos_ref[1], mate_ref)):
        w_ref[pl.ds(pl.multiple_of(c * 128, 128), 128), :] = ref[...]
    lane = lax.broadcasted_iota(jnp.int32, (PANEL, K), 1)
    row = lax.broadcasted_iota(jnp.int32, (PANEL, K), 0)
    for lo in range(0, K, PANEL):
        hi = lo + PANEL
        rest = w_ref[lo:hi, :]
        done, pivots = [], []
        for at in range(lo, hi, STEP):
            rest, found = eliminate(rest, at)
            done.append(rest[:STEP])
            pivots.append(found)
            rest = rest[STEP:]
        r = jnp.concatenate(done, axis=0)
        pivots = jnp.concatenate(pivots, axis=0)
        pivots = jnp.concatenate([pivots, pivots], axis=1)
        clean = jnp.where((lane < hi) & (lane > row + lo), 0.0, r)
        o_ref[lo:hi, :] = jnp.where(lane <= row + lo, clean, 0.0) * lax.rsqrt(pivots)
        if hi < K:
            start = hi // 128 * 128
            change = narrow_product((r / pivots)[:, start:], clean)
            rows = w_ref[hi:, :]
            lanes = lax.broadcasted_iota(jnp.int32, rows.shape, 1)
            kept = jnp.where((lanes >= lo) & (lanes < hi), 0.0, rows)
            w_ref[hi:, :] = kept - change[hi - start :]


def inverse_factor(pos, mine, mate):
    return call(inverse_kernel, f32s(K, K), 3, 0, 1 << 10,
                [pltpu.VMEM((K, K), F32)], smem=1)(pos, mine, mate)


def block_mask(n):
    rows = lax.broadcasted_iota(jnp.int32, (n, n), 0) // PADDED_RANK
    return rows == lax.broadcasted_iota(jnp.int32, (n, n), 1) // PADDED_RANK


def three_products(left, right, dims):
    left, right = split2(left), split2(right)
    return sum(
        lax.dot_general(left[i], right[j], (dims, ((), ())), preferred_element_type=F32)
        for i, j in THREE
    )


def couple(own, other, scale):
    small = jnp.where(block_mask(192), three_products(other, other, ((1,), (1,))), 0.0)
    return three_products(small, own, ((1,), (0,))) * scale


def first_kernel(*refs):
    left, right = refs[0:4], refs[4:8]
    scale_ref, c_ref, p_ref, q_ref = refs[8:]
    scale = scale_ref[...]
    p, q = (sum(r[...] for r in side) * scale for side in (left, right))
    c_ref[...] = couple(p, q, scale)
    p_ref[...] = p
    q_ref[...] = q


def normalised(pieces, linv_ref, scale):
    return lax.dot_general(sum(r[...] for r in pieces), linv_ref[...], (((1,), (1,)), ((), ())),
                           precision=HIGH, preferred_element_type=F32) * scale


def next_kernel(*refs):
    linv_ref, scale_ref, other_ref, c_ref, p_ref = refs[4:]
    scale = scale_ref[...]
    p = normalised(refs[:4], linv_ref, scale)
    c_ref[...] = couple(other_ref[...], p, scale)
    p_ref[...] = p


def last_kernel(*refs):
    linv_ref, scale_ref, q_ref = refs[4:]
    q_ref[...] = normalised(refs[:4], linv_ref, scale_ref[...])


def product(factors, at, blocks):
    a = jnp.concatenate([f[:, at : at + 384] for f in factors], axis=0)
    b = jnp.concatenate([b[...] for b in blocks], axis=0)
    return sum(jnp.dot(a, part, preferred_element_type=F32) for part in reversed(split2(b)))


def early_kernel(a0, a1, a2, a3, b0, b1, o_ref):
    o_ref[...] = product((a0, a1, a2, a3), 0, (b0, b1))


def late_kernel(side, pos_ref, a0, a1, a2, a3, b2, b3, part_ref, *refs):
    o_refs, m_ref = refs[:8], refs[8]
    total = part_ref[...] + product((a0, a1, a2, a3), 384, (b2, b3))
    for i, at in enumerate(row_places(side, pos_ref)):
        m_ref[at, :] = total[i * 256 : i * 256 + 256]
    for i, o_ref in enumerate(o_refs):
        c = pos_ref[1] if i < 4 else 1 - pos_ref[1]
        at = i // 4 * 512 + back(first_place(side, pos_ref, c), ORDER[i % 4]) * 128
        o_ref[...] = m_ref[pl.ds(pl.multiple_of(at, 128), 128), :]


def update(side, pos, straight, blocks):
    part = call(early_kernel, f32s(1024, 256), 6, 2 * 3072 << 16, 3 << 20)(*straight, *blocks[:2])
    return call(functools.partial(late_kernel, side), [f32s(128, 256)] * 8, 8, 2 * 3072 << 16,
                3 << 20, [pltpu.VMEM((1024, 256), F32)], smem=1)(
        pos, *straight, *blocks[2:], part
    )


def first_place(side, pos_ref, c):
    return jnp.where(c == 0, pos_ref[0], pos_ref[PLACE[side]])


def add_up(side, chunks):
    chunks = [mine + send(other, "core") for mine, other in zip(chunks[:4], chunks[4:])]
    chunk = sum(deliver(chunks, "x" + side))
    chunk = sum(exchange(chunk, side + "x"))
    return exchange(chunk, "x" + side)


def basis_kernel(rows_ref, linv_ref, o_ref):
    o_ref[...] = lax.dot_general(rows_ref[...], linv_ref[...], (((1,), (1,)), ((), ())),
                                 precision=HIGH, preferred_element_type=F32)


def basis_of(rows, linv):
    return call(basis_kernel, f32s(256, 256), 2, 12 << 24, 1 << 20)(rows, linv)


def cores_kernel(pos_ref, p_ref, *refs):
    blocks, o_ref, core_ref, sems = refs[:4], refs[4], refs[5], refs[6]
    mask = block_mask(192)
    copies = []
    for i, first in enumerate(ORDER):
        for j, second in enumerate(ORDER):
            source = chunk_at(pos_ref, first, second)
            wide = jnp.where(mask, jnp.concatenate([p_ref[source]] * 12, axis=0), 0.0)
            p_high, p_low = split2(wide)
            q_high, q_low = split2(blocks[i][j * 192 : j * 192 + 192, :])
            core = sum(
                jnp.dot(p, q, preferred_element_type=F32)
                for p, q in ((p_low, q_high), (p_high, q_low), (p_high, q_high))
            )
            at = i * RING + j
            core_ref[at] = core.reshape(12, 16, 256)
            copies.append(
                pltpu.make_async_copy(
                    core_ref.at[at], o_ref.at[pl.ds(source * 12, 12)], sems.at[at]
                )
            )
            copies[-1].start()
    for copy in copies:
        copy.wait()


def cores_of(pos, p_rows, blocks):
    return pl.pallas_call(
        cores_kernel,
        out_shape=f32s(192, 16, 256),
        in_specs=[SMEM] + [VMEM] * 5,
        out_specs=pl.BlockSpec(memory_space=pl.ANY),
        scratch_shapes=[
            pltpu.VMEM((16, 12, 16, 256), F32), pltpu.SemaphoreType.DMA((16,))
        ],
        compiler_params=PARAMS,
        cost_estimate=pl.CostEstimate(flops=1 << 30, bytes_accessed=6 << 20, transcendentals=0),
    )(pos, p_rows, *blocks)


def join_kernel(b0, b1, b2, b3, o_ref):
    for i, b in enumerate((b0, b1, b2, b3)):
        o_ref[i * 192 : (i + 1) * 192, :] = b[...]


def gather_all(value):
    joined = call(join_kernel, f32s(768, 256), 4, 0, 2 << 20)(*exchange(value, "zy"))
    return exchange(joined, "yz")


def refit(side, pos, straight, turned, coupling, last_sweep, beside=()):
    cross = CROSS[side] * 2
    *blocks, last = exchange(coupling, cross)
    last, *beside = lax.optimization_barrier((last, *beside))
    half = add_up(side, update(side, pos, straight, [*blocks, last]))
    rest = [send(chunk, "core") for chunk in half]
    piece = sum(exchange(gram(pos, rest, gram(pos, half)), cross))
    projected = project(side, pos, turned, half + rest, last_sweep)
    linv = inverse_factor(pos, piece, send(piece, "core"))
    return projected[4:], linv, deliver(projected[:4], cross), beside


def column_scale(ranks):
    positions = jnp.arange(PADDED_RANK, dtype=jnp.int32)
    live = positions[None, :] < ranks[:, None]
    factor = 4.0 / jnp.sqrt(ranks.astype(F32))
    return jnp.where(live, factor[:, None], F32(0.0)).reshape(-1, 1)


def shards(up, down, ranks, left, right):
    adapter, row = lax.axis_index("adapter"), lax.axis_index("row")
    c = adapter % 2
    pos = jnp.stack([adapter // 2, c, row // 4, row % 4]).astype(jnp.int32)
    scale = column_scale(lax.dynamic_slice_in_dim(ranks, row * 12, 12, 0))

    sides = lay_out(pieces_of(LEFT, pos, up, left), pieces_of(RIGHT, pos, down, right))
    (up_turned, up, left_chunks), (down_turned, down, right_chunks) = sides
    left_pieces = deliver(left_chunks, CROSS[LEFT] * 2)
    right_pieces = deliver(right_chunks, CROSS[RIGHT] * 2)
    side = f32s(192, 256)
    coupling, p, q = call(first_kernel, [side] * 3, 9, 1 << 28, 3 << 20)(
        *left_pieces, *right_pieces, scale
    )

    step = call(next_kernel, [side] * 2, 7, 1 << 29, 3 << 20)
    beside = ()
    for sweep in range(ITERS):
        last = sweep == ITERS - 1
        rows, linv, pieces, unused = refit(LEFT, pos, up, up_turned, coupling, last)
        coupling, p = step(*pieces, linv, scale, q)
        if last:
            beside = (basis_of(*rows, linv),)
            p_rows = lax.all_to_all(p.T.reshape(16, 16, 192), "row", 0, 0)
        rows, linv, pieces, beside = refit(
            RIGHT, pos, down, down_turned, coupling, last, beside
        )
        if not last:
            coupling, q = step(*pieces, linv, scale, p)
    q = call(last_kernel, side, 6, 1 << 28, 2 << 20)(*pieces, linv, scale)
    return beside[0], basis_of(*rows, linv), cores_of(pos, p_rows, gather_all(q))


def solution(mesh):
    return jax.shard_map(
        shards,
        mesh=mesh,
        in_specs=(
            P("row", "adapter"),
            P("row", "adapter"),
            P("adapter"),
            P("row", None),
            P("row", None),
        ),
        out_specs=(P("row", None), P("row", None), P("adapter", "row", None)),
        check_vma=False,
    )
```
